128 devices in a mesh: row: 8 (over z, core), col: 16 (over x, y).
Axes of the slice: x: 4, y: 4, z: 4, core: 2. Of those that a mesh axis runs over, the one named last changes fastest.
Arguments:
- images: bfloat16 [16384, 512], P(('row', 'col')), as said below
- texts: bfloat16 [16384, 512], P(('row', 'col')), as said below
- partner: int32 [16384], P('row'), may hold values from 0 to 16383, as said below
- log_scale: float32 [1], replicated, may hold values from 2.3 to 5.71
Outputs:
- image_grad: float32 [16384, 512], P(('row', 'col'))
- text_grad: float32 [16384, 512], P(('row', 'col'))
- loss: float32 [1], replicated
- temp_grad: float32 [1], replicated
The draws below stay inside these ranges and needn't reach their ends.
Inputs may be any that keep to these rules, and one draw needn't show every extreme that they name: `images`: finite image embeddings. `texts`: finite text embeddings. A permutation: every text is the partner of exactly one image.
All inputs are finite; a program needn't handle non-finite values.
Results may differ from the reference program's by a relative error of at most 0.017.
Values may be sent and summed in bfloat16 or wider, within the bound.
No kernel may reach another device: no remote copies, remote signals or barrier semaphores. Data moves between devices by JAX's collectives and lax.ppermute only.
A program may use at most 64 MiB of HBM per device.

```python
import math
import jax
import jax.numpy as jnp
from jax import lax

E = 512
ROWS_DEV = 128
BATCH = 16384
N_ROW = 8
N_COL = 16


def shared_text(key):
    return jax.random.normal(key, (BATCH, E), jnp.float32)


def pairing(key):
    return jax.random.permutation(jax.random.fold_in(key, 101), BATCH).astype(jnp.int32)


def draw_partner(key, part):
    return pairing(key)


def draw_texts(key, part):
    base = shared_text(key)
    return base.astype(jnp.bfloat16)


def draw_images(key, part):
    base = shared_text(key)
    order = pairing(key)
    key = jax.random.fold_in(key, 12)
    noise_rows = jax.random.normal(key, (BATCH, E), jnp.float32)
    ramp = jnp.arange(BATCH, dtype=jnp.float32) / max(BATCH - 1, 1)
    align = 1.0 - ramp
    values = align[:, None] * base[order] + (1.0 - align)[:, None] * noise_rows
    return values.astype(jnp.bfloat16)


def draw_log_scale(key, part):
    key = jax.random.fold_in(key, 13)
    return jax.random.uniform(key, (1,), jnp.float32, math.log(10.0), math.log(60.0))


def setup_inputs(seed: int = 0) -> dict:
    seeds = jax.random.split(jax.random.key(seed), 5)
    return {
        "images": draw_images(jax.random.fold_in(seeds[4], 71), 0),
        "texts": draw_texts(jax.random.fold_in(seeds[4], 71), 0),
        "partner": draw_partner(jax.random.fold_in(seeds[4], 71), 0),
        "log_scale": draw_log_scale(jax.random.fold_in(seeds[4], 71), 0),
    }


def unit_rows(values):
    widened = values.astype(jnp.float32)
    inverse = lax.rsqrt(lax.optimization_barrier(jnp.sum(widened * widened, axis=1, keepdims=True)) + 1e-06)
    return (widened * inverse, inverse)

def through_norm(grad_unit, unit_values, inverse):
    return inverse * (grad_unit - unit_values * lax.optimization_barrier(jnp.sum(unit_values * grad_unit, axis=1, keepdims=True)))

def reference(images, texts, partner, log_scale):
    unit_img, inv_img = unit_rows(images)
    unit_txt, inv_txt = unit_rows(texts)
    img_bf = unit_img.astype(jnp.bfloat16)
    txt_bf = unit_txt.astype(jnp.bfloat16)
    temp_scale = jnp.exp(log_scale[0])
    block_rows = min(1024, BATCH)
    count_blocks = BATCH // block_rows
    text_ids = jnp.arange(BATCH, dtype=jnp.int32)
    row_blocks = img_bf.reshape(count_blocks, block_rows, E)
    pair_blocks = partner.reshape(count_blocks, block_rows)

    def logits_of(row_piece):
        return temp_scale * jnp.dot(row_piece, txt_bf.T, preferred_element_type=jnp.float32)

    def forward(running, inputs):
        row_piece, targets = inputs
        logits = logits_of(row_piece)
        matched = targets[:, None] == text_ids[None, :]
        picked = jnp.where(matched, logits, 0.0)
        row_high = lax.optimization_barrier(jnp.max(logits, axis=1))
        weights = jnp.exp(logits - row_high[:, None])
        row_out = (row_high, lax.optimization_barrier(jnp.sum(weights, axis=1)), lax.optimization_barrier(jnp.sum(weights * logits, axis=1)), lax.optimization_barrier(jnp.sum(picked, axis=1)))
        col_high = jnp.maximum(running[0], lax.optimization_barrier(jnp.max(logits, axis=0)))
        rescale = jnp.exp(running[0] - col_high)
        col_weights = jnp.exp(logits - col_high[None, :])
        updated = (col_high, running[1] * rescale + lax.optimization_barrier(jnp.sum(col_weights, axis=0)), running[2] * rescale + lax.optimization_barrier(jnp.sum(col_weights * logits, axis=0)))
        return (updated, row_out)
    start_state = (jnp.full((BATCH,), -jnp.inf, dtype=jnp.float32), jnp.zeros((BATCH,), jnp.float32), jnp.zeros((BATCH,), jnp.float32))
    col_part, row_part = lax.scan(forward, start_state, (row_blocks, pair_blocks))
    row_high, row_sum, row_weighted, row_pick = [piece.reshape(BATCH) for piece in row_part]
    col_high, col_sum, col_weighted = col_part
    row_logsum = row_high + jnp.log(row_sum)
    col_logsum = col_high + jnp.log(col_sum)
    pick_total = jnp.sum(row_pick)
    loss = ((jnp.sum(row_logsum) + jnp.sum(col_logsum) - 2.0 * pick_total) / (2 * BATCH)).reshape(1)
    temp_grad = ((jnp.sum(row_weighted / row_sum) + jnp.sum(col_weighted / col_sum) - 2.0 * pick_total) / (2 * BATCH)).reshape(1)
    group_rows = ROWS_DEV * N_COL
    txt_groups = txt_bf.reshape(N_ROW, N_COL, ROWS_DEV, E).astype(jnp.float32)

    def backward(running, inputs):
        row_piece, targets, logsum_piece = inputs
        logits = logits_of(row_piece)
        matched = jnp.where(targets[:, None] == text_ids[None, :], 1.0, 0.0)
        soft = 0.5 * (jnp.exp(logits - logsum_piece[:, None]) + jnp.exp(logits - col_logsum[None, :]))
        dlogit = (soft - matched).astype(jnp.bfloat16)
        tile_groups = dlogit.astype(jnp.float32).reshape(group_rows, N_ROW, N_COL, ROWS_DEV)
        partial_img = temp_scale * jnp.einsum('iack,acke->ice', tile_groups, txt_groups)
        img_part = lax.optimization_barrier(jnp.sum(partial_img.astype(jnp.bfloat16).astype(jnp.float32), axis=1))
        partial_txt = temp_scale * jnp.dot(dlogit.T, row_piece, preferred_element_type=jnp.float32)
        running = running + partial_txt.astype(jnp.bfloat16).astype(jnp.float32)
        return (running, img_part)
    txt_unit_grad, img_parts = lax.scan(backward, jnp.zeros((BATCH, E), jnp.float32), (img_bf.reshape(N_ROW, group_rows, E), partner.reshape(N_ROW, group_rows), row_logsum.reshape(N_ROW, group_rows)))
    image_grad = through_norm(img_parts.reshape(BATCH, E), unit_img, inv_img)
    text_grad = through_norm(txt_unit_grad, unit_txt, inv_txt)
    return (image_grad, text_grad, loss, temp_grad)
```

```python
import functools

import jax
import jax.numpy as jnp
from jax import lax
from jax.experimental import pallas as pl
from jax.experimental.pallas import tpu as pltpu
from jax.sharding import PartitionSpec as P

ROWS = 128
WIDTH = 512
QUAD = 4 * ROWS
EXTRA = 16
OFFS = (0, 2, 1, 3)
LOG2E = 1.4426950408889634
LN2 = 0.6931471805599453
RC = ("row", "col")
F32 = jnp.float32
BF16 = jnp.bfloat16
VMEM = pl.BlockSpec(memory_space=pltpu.VMEM)
SMEM = pl.BlockSpec(memory_space=pltpu.SMEM)
PARAMS = pltpu.CompilerParams(vmem_limit_bytes=40 * 1024 * 1024)


def device(z, k, x, y):
    return (z * 2 + k) * 16 + x * 4 + y


def shifted(value, move):
    pairs = []
    for z in range(4):
        for k in range(2):
            for x in range(4):
                for y in range(4):
                    pairs.append((device(z, k, x, y), device(*move(z, k, x, y))))
    return lax.ppermute(value, RC, pairs)


def ring_a(by):
    return lambda z, k, x, y: (z, k, x, (y + by) % 4) if k else (z, k, (x + by) % 4, y)


def ring_b(by):
    return lambda z, k, x, y: (z, k, (x + by) % 4, y) if k else (z, k, x, (y + by) % 4)


def ring_z(by):
    return lambda z, k, x, y: ((z + by) % 4, k, x, y)


def other_core(z, k, x, y):
    return (z, 1 - k, x, y)


def call(kernel, outs, *args, specs=None, cost=None, scratch=()):
    return pl.pallas_call(
        kernel,
        out_shape=outs,
        in_specs=specs or [VMEM] * len(args),
        out_specs=jax.tree.map(lambda o: VMEM, outs),
        scratch_shapes=scratch,
        compiler_params=PARAMS,
        cost_estimate=cost,
    )(*args)


def shape(dims, dtype):
    return jax.ShapeDtypeStruct(dims, dtype)


def unit_rows(values):
    widened = values.astype(F32)
    inverse = lax.rsqrt(jnp.sum(widened * widened, axis=1, keepdims=True) + 1e-06)
    return widened * inverse, inverse


def unit_kernel(img_ref, txt_ref, img_out, txt_out):
    img_out[...] = unit_rows(img_ref[...])[0].astype(BF16)
    txt_out[...] = unit_rows(txt_ref[...])[0].astype(BF16)


def places(ids_ref):
    row, col = ids_ref[0], ids_ref[1]
    z, k, x, y = row // 2, row % 2, col // 4, col % 4
    pos_a = jnp.where(k == 0, x, y)
    pos_b = jnp.where(k == 0, y, x)

    def col_of(q, a):
        in_b = (pos_b + 4 - OFFS[q]) % 4
        in_a = (pos_a + 4 - OFFS[a]) % 4
        return jnp.where(k == 0, in_a * 4 + in_b, in_b * 4 + in_a)

    def row_of(j, t):
        return (z + 4 - OFFS[t]) % 4 * 2 + (k if j == 0 else 1 - k)

    return col_of, row_of


def to_lanes(column):
    return jnp.transpose(jnp.broadcast_to(column, (ROWS, ROWS)))[0:1, :]


def logits2(rows, t_refs, scale2):
    parts = [
        lax.dot_general(rows, t[...], (((1,), (1,)), ((), ())), preferred_element_type=F32)
        for t in t_refs
    ]
    return jnp.concatenate(parts, axis=1) * scale2


CHUNK = 256


def forward_kernel(ids_ref, scale_ref, pos_ref, i0, i1, i2, i3, t0, t1, row_out, col_out, col_state):
    scale2 = scale_ref[0] * LOG2E
    col_of, row_of = places(ids_ref)
    lanes = lax.broadcasted_iota(jnp.int32, (CHUNK, 8 * ROWS), 1)
    col_state[0:1, :] = jnp.full((1, 8 * ROWS), -jnp.inf, F32)
    col_state[1:3, :] = jnp.zeros((2, 8 * ROWS), F32)
    picked = jnp.zeros((1, 8 * ROWS), F32)
    for q, rows_ref in enumerate((i0, i1, i2, i3)):
        for h in range(QUAD // CHUNK):
            logits = logits2(rows_ref[h * CHUNK : (h + 1) * CHUNK, :], (t0, t1), scale2)
            high = jnp.max(logits, axis=1, keepdims=True)
            weights = jnp.exp2(logits - high)
            total = jnp.sum(weights, axis=1, keepdims=True)
            mean = jnp.sum(weights * logits, axis=1, keepdims=True) / total
            lse = high + jnp.log2(total)
            pos = []
            for b in range(CHUNK // ROWS):
                place = col_of(q, h * (CHUNK // ROWS) + b)
                row_out[pl.ds(place, 1), :] = to_lanes(lse[b * ROWS : (b + 1) * ROWS])
                row_out[pl.ds(16 + place, 1), :] = to_lanes(mean[b * ROWS : (b + 1) * ROWS])
                pos.append(pos_ref[pl.ds(pl.multiple_of(place * ROWS, ROWS), ROWS), :])
            pos = jnp.concatenate(pos, axis=0)
            pos = jnp.concatenate([pos] * 8, axis=1)
            picked += jnp.sum(jnp.where(pos == lanes, logits, 0.0), axis=0, keepdims=True)
            old = col_state[0:1, :]
            col_high = jnp.maximum(old, jnp.max(logits, axis=0, keepdims=True))
            rescale = jnp.exp2(old - col_high)
            col_weights = jnp.exp2(logits - col_high)
            col_state[0:1, :] = col_high
            col_state[1:2, :] = col_state[1:2, :] * rescale + jnp.sum(col_weights, axis=0, keepdims=True)
            col_state[2:3, :] = col_state[2:3, :] * rescale + jnp.sum(
                col_weights * logits, axis=0, keepdims=True
            )
    row_out[32:40, :] = jnp.broadcast_to(jnp.sum(picked, axis=1, keepdims=True), (8, ROWS))
    col_lse = col_state[0:1, :] + jnp.log2(col_state[1:2, :])
    col_mean = col_state[2:3, :] / col_state[1:2, :]
    for j in range(2):
        for t in range(4):
            at = (j * 4 + t) * ROWS
            place = row_of(j, t)
            col_out[pl.ds(place, 1), :] = col_lse[:, at : at + ROWS]
            col_out[pl.ds(8 + place, 1), :] = col_mean[:, at : at + ROWS]


def combined(refs, count):
    parts = [r[0:count, :] for r in refs]
    means = [r[count : 2 * count, :] for r in refs]
    high = functools.reduce(jnp.maximum, parts)
    weights = [jnp.exp2(p - high) for p in parts]
    total = sum(weights)
    mean = sum(w * m for w, m in zip(weights, means)) / total
    return high + jnp.log2(total), mean


def combine_kernel(r0, r1, r2, r3, c0, c1, c2, c3, row_out, col_out):
    row_out[0:16, :], row_out[16:32, :] = combined((r0, r1, r2, r3), 16)
    row_out[32:40, :] = r0[32:40, :] + r1[32:40, :] + r2[32:40, :] + r3[32:40, :]
    col_out[0:8, :], col_out[8:16, :] = combined((c0, c1, c2, c3), 8)


def in_parts(first, second):
    lane = lax.broadcasted_iota(jnp.int32, (EXTRA, WIDTH), 1)
    part = lax.broadcasted_iota(jnp.int32, (EXTRA, WIDTH), 0)
    value = jnp.where(lane == 0, first, jnp.where(lane == 1, second, 0.0))
    high = value.astype(BF16)
    rest = value - high.astype(F32)
    mid = rest.astype(BF16)
    low = (rest - mid.astype(F32)).astype(BF16)
    zero = jnp.zeros((EXTRA, WIDTH), F32)
    out = jnp.where(part == 0, high.astype(F32), zero)
    out = jnp.where(part == 1, mid.astype(F32), out)
    return jnp.where(part == 2, low.astype(F32), out).astype(BF16)


def backward_kernel(
    ids_ref, scale_ref, pos_ref, r0, r1, r2, r3, c0, c1, i0, i1, i2, i3, t0, t1,
    g0, g1, g2, g3, h0, h1, row_shift, col_shift, acc,
):
    scale = scale_ref[0]
    scale2 = scale * LOG2E
    col_of, row_of = places(ids_ref)
    row_lse, row_mean = combined((r0, r1, r2, r3), 16)
    col_lse, col_mean = combined((c0, c1), 8)
    picked = r0[32:33, 0:1] + r1[32:33, 0:1] + r2[32:33, 0:1] + r3[32:33, 0:1]
    row_shift[...] = row_lse + 1.0
    col_shift[...] = col_lse + 1.0
    row_tail = in_parts(
        (jnp.sum(row_lse, keepdims=True) - 2.0 * picked) * LN2,
        (jnp.sum(row_mean, keepdims=True) - 2.0 * picked) * LN2,
    )
    col_tail = in_parts(jnp.sum(col_lse, keepdims=True) * LN2, jnp.sum(col_mean, keepdims=True) * LN2)
    columns = jnp.concatenate(
        [col_shift[pl.ds(row_of(j, t), 1), :] for j in range(2) for t in range(4)], axis=1
    )
    lanes = lax.broadcasted_iota(jnp.int32, (ROWS, 8 * ROWS), 1)
    for q, (rows_ref, g_ref) in enumerate(zip((i0, i1, i2, i3), (g0, g1, g2, g3))):
        for h in range(QUAD // CHUNK):
            rows = rows_ref[h * CHUNK : (h + 1) * CHUNK, :]
            logits = logits2(rows, (t0, t1), scale2)
            pieces = []
            for b in range(CHUNK // ROWS):
                place = col_of(q, h * (CHUNK // ROWS) + b)
                shift = jnp.transpose(
                    jnp.broadcast_to(row_shift[pl.ds(place, 1), :], (ROWS, ROWS))
                )
                pos = pos_ref[pl.ds(pl.multiple_of(place * ROWS, ROWS), ROWS), :]
                shift = jnp.concatenate([shift] * 8, axis=1)
                pos = jnp.concatenate([pos] * 8, axis=1)
                part = logits[b * ROWS : (b + 1) * ROWS]
                soft = jnp.exp2(part - shift) + jnp.exp2(part - columns)
                pieces.append(jnp.where(pos == lanes, soft - 1.0, soft).astype(BF16))
            grad = jnp.concatenate(pieces, axis=0)
            product = jnp.dot(grad[:, :QUAD], t0[...], preferred_element_type=F32)
            product += jnp.dot(grad[:, QUAD:], t1[...], preferred_element_type=F32)
            g_ref[h * CHUNK : (h + 1) * CHUNK, :] = (scale * product).astype(BF16)
            update = lax.dot_general(grad, rows, (((0,), (0,)), ((), ())), preferred_element_type=F32)
            if q == 0 and h == 0:
                acc[...] = update
            else:
                acc[...] += update
        g_ref[QUAD : QUAD + EXTRA, :] = col_tail
    h0[0:QUAD, :] = (scale * acc[0:QUAD, :]).astype(BF16)
    h1[0:QUAD, :] = (scale * acc[QUAD : 2 * QUAD, :]).astype(BF16)
    h0[QUAD : QUAD + EXTRA, :] = row_tail
    h1[QUAD : QUAD + EXTRA, :] = row_tail


def tail_sum(refs, first):
    total = sum(r[first : first + EXTRA, :].astype(F32) for r in refs)
    total = jnp.sum(total, axis=0, keepdims=True)
    return total[:, 0:1], total[:, 1:2]


def partial_kernel(*refs):
    sources, outs = refs[:-4], refs[-4:]
    tail = in_parts(*tail_sum(sources, QUAD))
    for t, out in enumerate(outs):
        rows = slice(t * ROWS, (t + 1) * ROWS)
        out[0:ROWS, :] = sum(r[rows, :].astype(F32) for r in sources).astype(BF16)
        out[ROWS : ROWS + EXTRA, :] = tail


def finish_kernel(batch, img_ref, txt_ref, a0, a1, a2, a3, b0, b1, b2, b3, img_out, txt_out, loss_out, temp_out):
    for raw, parts, out in ((img_ref, (a0, a1, a2, a3), img_out), (txt_ref, (b0, b1, b2, b3), txt_out)):
        unit, inverse = unit_rows(raw[...])
        grad = sum(p[0:ROWS, :].astype(F32) for p in parts)
        out[...] = inverse * (grad - unit * jnp.sum(unit * grad, axis=1, keepdims=True))
    cols = tail_sum((a0, a1, a2, a3), ROWS)
    rows = tail_sum((b0, b1, b2, b3), ROWS)
    loss_out[0] = jnp.sum(cols[0] + rows[0]) / (2 * batch)
    temp_out[0] = jnp.sum(cols[1] + rows[1]) / (2 * batch)


def gathered(value, moves):
    return [value] + [shifted(value, moves(by)) for by in OFFS[1:]]


def scattered(parts, moves):
    return [parts[0]] + [shifted(p, moves(-by)) for p, by in zip(parts[1:], OFFS[1:])]


def on_device(images, texts, partner, log_scale):
    row, col = lax.axis_index("row"), lax.axis_index("col")
    ids = jnp.stack([row, col]).astype(jnp.int32)
    scale = jnp.exp(log_scale)
    unit_img, unit_txt = call(unit_kernel, [shape((ROWS, WIDTH), BF16)] * 2, images, texts)
    txt0 = jnp.concatenate(gathered(unit_txt, ring_z), axis=0)
    img_own = jnp.concatenate(gathered(unit_img, ring_a), axis=0)
    txt1 = shifted(txt0, other_core)
    imgs = gathered(img_own, ring_b)

    owner = partner // (16 * ROWS)
    steps = (row // 2 - owner // 2) % 4
    slot = steps % 2 * 2 + steps // 2
    core = jnp.where(owner % 2 == row % 2, 0, 1)
    pos = (core * 4 + slot) * ROWS + partner % ROWS
    pos = jnp.where(partner // ROWS % 16 == col, pos, -1)
    pos = jnp.broadcast_to(pos[:, None], (16 * ROWS, ROWS))

    row_stat, col_stat = call(
        forward_kernel,
        [shape((40, ROWS), F32), shape((16, ROWS), F32)],
        ids, scale, pos, *imgs, txt0, txt1,
        specs=[SMEM, SMEM] + [VMEM] * 7,
        scratch=[pltpu.VMEM((8, 8 * ROWS), F32)],
    )
    row_stat, col_stat = call(
        combine_kernel,
        [shape((40, ROWS), F32), shape((16, ROWS), F32)],
        *gathered(row_stat, ring_a), *gathered(col_stat, ring_z),
    )
    row_stats = gathered(row_stat, ring_b)
    col_stats = [col_stat, shifted(col_stat, other_core)]

    sent = shape((QUAD + EXTRA, WIDTH), BF16)
    grads = call(
        backward_kernel,
        [sent] * 6,
        ids, scale, pos, *row_stats, *col_stats, *imgs, txt0, txt1,
        specs=[SMEM, SMEM] + [VMEM] * 13,
        scratch=[
            pltpu.VMEM((16, ROWS), F32),
            pltpu.VMEM((8, ROWS), F32),
            pltpu.VMEM((8 * ROWS, WIDTH), F32),
        ],
    )
    small = [shape((ROWS + EXTRA, WIDTH), BF16)] * 4
    txt_parts = call(partial_kernel, small, grads[4], shifted(grads[5], other_core))
    img_parts = call(partial_kernel, small, *scattered(grads[:4], ring_b))
    txt_parts = scattered(txt_parts, ring_z)
    img_parts = scattered(img_parts, ring_a)
    whole = shape((ROWS, WIDTH), F32)
    one = shape((1,), F32)
    return pl.pallas_call(
        functools.partial(finish_kernel, 128 * ROWS),
        out_shape=(whole, whole, one, one),
        in_specs=[VMEM] * 10,
        out_specs=(VMEM, VMEM, SMEM, SMEM),
        compiler_params=PARAMS,
    )(images, texts, *img_parts, *txt_parts)


def solution(mesh):
    placed = (P(("row", "col"), None), P(("row", "col"), None), P("row"), P())
    return jax.shard_map(
        on_device,
        mesh=mesh,
        in_specs=placed,
        out_specs=(P(("row", "col"), None), P(("row", "col"), None), P(), P()),
        check_vma=False,
    )
```

```python
import functools

import jax
import jax.numpy as jnp
from jax import lax
from jax.experimental import pallas as pl
from jax.experimental.pallas import tpu as pltpu
from jax.sharding import PartitionSpec as P

ROWS = 128
WIDTH = 512
QUAD = 4 * ROWS
EXTRA = 16
OFFS = (0, 1, 3, 2)
LOG2E = 1.4426950408889634
LN2 = 0.6931471805599453
RC = ("row", "col")
F32 = jnp.float32
BF16 = jnp.bfloat16
VMEM = pl.BlockSpec(memory_space=pltpu.VMEM)
SMEM = pl.BlockSpec(memory_space=pltpu.SMEM)
PARAMS = pltpu.CompilerParams(vmem_limit_bytes=24 * 1024 * 1024)


def device(z, k, x, y):
    return (z * 2 + k) * 16 + x * 4 + y


def shifted(value, move):
    pairs = []
    for z in range(4):
        for k in range(2):
            for x in range(4):
                for y in range(4):
                    pairs.append((device(z, k, x, y), device(*move(z, k, x, y))))
    return lax.ppermute(value, RC, pairs)


def ring_a(by):
    return lambda z, k, x, y: (z, k, x, (y + by) % 4) if k else (z, k, (x + by) % 4, y)


def ring_b(by):
    return lambda z, k, x, y: (z, k, (x + by) % 4, y) if k else (z, k, x, (y + by) % 4)


def ring_z(by):
    return lambda z, k, x, y: ((z + by) % 4, k, x, y)


def other_core(z, k, x, y):
    return (z, 1 - k, x, y)


def call(kernel, outs, *args, specs=None, cost=None, scratch=()):
    return pl.pallas_call(
        kernel,
        out_shape=outs,
        in_specs=specs or [VMEM] * len(args),
        out_specs=jax.tree.map(lambda o: VMEM, outs),
        scratch_shapes=scratch,
        compiler_params=PARAMS,
        cost_estimate=cost,
    )(*args)


def shape(dims, dtype):
    return jax.ShapeDtypeStruct(dims, dtype)


def unit_rows(values):
    widened = values.astype(F32)
    inverse = lax.rsqrt(jnp.sum(widened * widened, axis=1, keepdims=True) + 1e-06)
    return widened * inverse, inverse


def unit_kernel(raw_ref, *refs):
    refs[-1][...] = unit_rows(raw_ref[...])[0].astype(BF16)


def after_kernel(*refs):
    refs[-1][...] = jnp.zeros_like(refs[-1])


def places(ids_ref):
    row, col = ids_ref[0], ids_ref[1]
    z, k, x, y = row // 2, row % 2, col // 4, col % 4
    pos_a = jnp.where(k == 0, x, y)
    pos_b = jnp.where(k == 0, y, x)

    def col_of(q, a):
        in_b = (pos_b + 4 - OFFS[q]) % 4
        in_a = (pos_a + 4 - OFFS[a]) % 4
        return jnp.where(k == 0, in_a * 4 + in_b, in_b * 4 + in_a)

    def row_of(j, t):
        return (z + 4 - OFFS[t]) % 4 * 2 + (k if j == 0 else 1 - k)

    return col_of, row_of


def to_lanes(column):
    return jnp.transpose(jnp.broadcast_to(column, (ROWS, ROWS)))[0:1, :]


def logits2(rows, t0, t1, scale2):
    parts = [
        lax.dot_general(rows, t[...], (((1,), (1,)), ((), ())), preferred_element_type=F32)
        for t in (t0, t1)
    ]
    return jnp.concatenate(parts, axis=1) * scale2


CHUNK = 256


def forward_kernel(
    ids_ref, scale_ref, pos_ref, i0, i1, i2, i3, t0, t1, _, row_out, col_out
):
    scale2 = scale_ref[0] * LOG2E
    col_of, row_of = places(ids_ref)
    lanes = lax.broadcasted_iota(jnp.int32, (CHUNK, 8 * ROWS), 1)
    col_high = jnp.full((1, 8 * ROWS), -jnp.inf, F32)
    col_total = col_weighted = picked = jnp.zeros((1, 8 * ROWS), F32)
    for q, rows_ref in enumerate((i0, i1, i2, i3)):
        for h in range(QUAD // CHUNK):
            logits = logits2(rows_ref[h * CHUNK : (h + 1) * CHUNK, :], t0, t1, scale2)
            high = jnp.max(logits, axis=1, keepdims=True)
            weights = jnp.exp2(logits - high)
            total = jnp.sum(weights, axis=1, keepdims=True)
            mean = jnp.sum(weights * logits, axis=1, keepdims=True) / total
            lse = high + jnp.log2(total)
            pos = []
            for b in range(CHUNK // ROWS):
                place = col_of(q, h * (CHUNK // ROWS) + b)
                row_out[pl.ds(place, 1), :] = to_lanes(lse[b * ROWS : (b + 1) * ROWS])
                row_out[pl.ds(16 + place, 1), :] = to_lanes(mean[b * ROWS : (b + 1) * ROWS])
                pos.append(pos_ref[pl.ds(pl.multiple_of(place * ROWS, ROWS), ROWS), :])
            pos = jnp.concatenate(pos, axis=0)
            pos = jnp.concatenate([pos] * 8, axis=1)
            picked += jnp.sum(jnp.where(pos == lanes, logits, 0.0), axis=0, keepdims=True)
            old = col_high
            col_high = jnp.maximum(old, jnp.max(logits, axis=0, keepdims=True))
            rescale = jnp.exp2(old - col_high)
            weights = jnp.exp2(logits - col_high)
            col_total = col_total * rescale + jnp.sum(weights, axis=0, keepdims=True)
            col_weighted = col_weighted * rescale + jnp.sum(weights * logits, axis=0, keepdims=True)
    row_out[32:40, :] = jnp.broadcast_to(jnp.sum(picked, axis=1, keepdims=True), (8, ROWS))
    col_lse = col_high + jnp.log2(col_total)
    col_mean = col_weighted / col_total
    for j in range(2):
        for t in range(4):
            at = (j * 4 + t) * ROWS
            place = row_of(j, t)
            col_out[pl.ds(place, 1), :] = col_lse[:, at : at + ROWS]
            col_out[pl.ds(8 + place, 1), :] = col_mean[:, at : at + ROWS]


def merged(parts, count):
    lse = [p[0:count, :] for p in parts]
    high = functools.reduce(jnp.maximum, lse)
    weights = [jnp.exp2(p - high) for p in lse]
    total = sum(weights)
    mean = sum(w * p[count : 2 * count, :] for w, p in zip(weights, parts)) / total
    return high + jnp.log2(total), mean


def merge_kernel(r0, r1, r2, r3, c0, c1, row_out, col_out):
    refs = (r0, r1, r2, r3)
    row_out[0:16, :], row_out[16:32, :] = merged(refs, 16)
    row_out[32:40, :] = sum(r[32:40, :] for r in refs)
    col_out[0:8, :], col_out[8:16, :] = merged((c0, c1), 8)


def in_parts(first, second):
    lane = lax.broadcasted_iota(jnp.int32, (EXTRA, WIDTH), 1)
    part = lax.broadcasted_iota(jnp.int32, (EXTRA, WIDTH), 0)
    value = jnp.where(lane == 0, first, jnp.where(lane == 1, second, 0.0))
    high = value.astype(BF16)
    rest = value - high.astype(F32)
    mid = rest.astype(BF16)
    low = (rest - mid.astype(F32)).astype(BF16)
    zero = jnp.zeros((EXTRA, WIDTH), F32)
    out = jnp.where(part == 0, high.astype(F32), zero)
    out = jnp.where(part == 1, mid.astype(F32), out)
    return jnp.where(part == 2, low.astype(F32), out).astype(BF16)


def shifts_kernel(ids_ref, row_ref, c0, c1, row_shift, columns, row_tail, col_tail, col_shift):
    _, row_of = places(ids_ref)
    row_lse, row_mean = row_ref[0:16, :], row_ref[16:32, :]
    col_lse, col_mean = merged((c0, c1), 8)
    picked = row_ref[32:33, 0:1]
    row_shift[...] = row_lse + 1.0
    col_shift[...] = col_lse + 1.0
    columns[...] = jnp.concatenate(
        [col_shift[pl.ds(row_of(j, t), 1), :] for j in range(2) for t in range(4)], axis=1
    )
    row_tail[...] = in_parts(
        (jnp.sum(row_lse, keepdims=True) - 2.0 * picked) * LN2,
        (jnp.sum(row_mean, keepdims=True) - 2.0 * picked) * LN2,
    )
    col_tail[...] = in_parts(
        jnp.sum(col_lse, keepdims=True) * LN2, jnp.sum(col_mean, keepdims=True) * LN2
    )


def dlogit_kernel(
    ids_ref, scale_ref, pos_ref, row_shift, col_shift, row_tail, i0, i1, i2, i3, t0, t1,
    d0, d1, d2, d3, h0, h1, acc,
):
    scale = scale_ref[0]
    scale2 = scale * LOG2E
    col_of, row_of = places(ids_ref)
    columns = col_shift[...]
    lanes = lax.broadcasted_iota(jnp.int32, (ROWS, 8 * ROWS), 1)
    for q, (rows_ref, d_ref) in enumerate(zip((i0, i1, i2, i3), (d0, d1, d2, d3))):
        for h in range(QUAD // CHUNK):
            rows = rows_ref[h * CHUNK : (h + 1) * CHUNK, :]
            logits = logits2(rows, t0, t1, scale2)
            pieces = []
            for b in range(CHUNK // ROWS):
                place = col_of(q, h * (CHUNK // ROWS) + b)
                shift = jnp.transpose(jnp.broadcast_to(row_shift[pl.ds(place, 1), :], (ROWS, ROWS)))
                pos = pos_ref[pl.ds(pl.multiple_of(place * ROWS, ROWS), ROWS), :]
                shift = jnp.concatenate([shift] * 8, axis=1)
                pos = jnp.concatenate([pos] * 8, axis=1)
                part = logits[b * ROWS : (b + 1) * ROWS]
                soft = jnp.exp2(part - shift) + jnp.exp2(part - columns)
                pieces.append(jnp.where(pos == lanes, soft - 1.0, soft).astype(BF16))
            grad = jnp.concatenate(pieces, axis=0)
            d_ref[h * CHUNK : (h + 1) * CHUNK, :] = grad
            update = lax.dot_general(
                grad, rows, (((0,), (0,)), ((), ())), preferred_element_type=F32
            )
            if q == 0 and h == 0:
                acc[...] = update
            else:
                acc[...] += update
    for j, out in enumerate((h0, h1)):
        out[0:QUAD, :] = (scale * acc[j * QUAD : (j + 1) * QUAD, :]).astype(BF16)
        out[QUAD : QUAD + EXTRA, :] = row_tail[...]


def images_kernel(scale_ref, col_tail, t0, t1, d_ref, g_ref):
    product = jnp.dot(d_ref[:, :QUAD], t0[...], preferred_element_type=F32)
    product += jnp.dot(d_ref[:, QUAD:], t1[...], preferred_element_type=F32)
    g_ref[0:QUAD, :] = (scale_ref[0] * product).astype(BF16)
    g_ref[QUAD : QUAD + EXTRA, :] = col_tail[...]


def tail_sum(refs, first):
    total = sum(r[first : first + EXTRA, :].astype(F32) for r in refs)
    total = jnp.sum(total, axis=0, keepdims=True)
    return total[:, 0:1], total[:, 1:2]


def partial_kernel(*refs):
    sources, outs = refs[:-4], refs[-4:]
    tail = in_parts(*tail_sum(sources, QUAD))
    for t, out in enumerate(outs):
        rows = slice(t * ROWS, (t + 1) * ROWS)
        out[0:ROWS, :] = sum(r[rows, :].astype(F32) for r in sources).astype(BF16)
        out[ROWS : ROWS + EXTRA, :] = tail


def finish_kernel(batch, img_ref, txt_ref, a0, a1, a2, a3, b0, b1, b2, b3, img_out, txt_out, loss_out, temp_out):
    for raw, parts, out in ((img_ref, (a0, a1, a2, a3), img_out), (txt_ref, (b0, b1, b2, b3), txt_out)):
        unit, inverse = unit_rows(raw[...])
        grad = sum(p[0:ROWS, :].astype(F32) for p in parts)
        out[...] = inverse * (grad - unit * jnp.sum(unit * grad, axis=1, keepdims=True))
    cols = tail_sum((a0, a1, a2, a3), ROWS)
    rows = tail_sum((b0, b1, b2, b3), ROWS)
    loss_out[0] = jnp.sum(cols[0] + rows[0]) / (2 * batch)
    temp_out[0] = jnp.sum(cols[1] + rows[1]) / (2 * batch)


def gathered(value, moves):
    return [value] + [shifted(value, moves(by)) for by in OFFS[1:]]


def scattered(parts, moves):
    return [parts[0]] + [shifted(p, moves(-by)) for p, by in zip(parts[1:], OFFS[1:])]


def across(place, far):
    return 3 - place if far else place ^ 1


def pair_z(far):
    return lambda z, k, x, y: (across(z, far), k, x, y)


def on_device(images, texts, partner, log_scale):
    row, col = lax.axis_index("row"), lax.axis_index("col")
    ids = jnp.stack([row, col]).astype(jnp.int32)
    scale = jnp.exp(log_scale)
    unit = shape((ROWS, WIDTH), BF16)
    anywhere = pl.BlockSpec(memory_space=pl.ANY)
    anywhere = pl.BlockSpec(memory_space=pl.ANY)
    token = shape((8, ROWS), F32)
    unit_img = call(unit_kernel, unit, images)
    unit_txt = call(unit_kernel, unit, texts, unit_img, specs=[VMEM, anywhere])
    img_own = jnp.concatenate(gathered(unit_img, ring_a), axis=0)
    txt0 = jnp.concatenate(gathered(unit_txt, ring_z), axis=0)
    imgs = gathered(img_own, ring_b)
    txt1 = shifted(txt0, other_core)
    arrived = call(after_kernel, token, *imgs[1:], specs=[VMEM] * 3)

    owner = partner // (16 * ROWS)
    steps = (row // 2 - owner // 2) % 4
    slot = steps ^ (steps // 2)
    core = jnp.where(owner % 2 == row % 2, 0, 1)
    pos = (core * 4 + slot) * ROWS + partner % ROWS
    pos = jnp.where(partner // ROWS % 16 == col, pos, -1)
    pos = jnp.broadcast_to(pos[:, None], (16 * ROWS, ROWS))

    row_shape = shape((40, ROWS), F32)
    common = (ids, scale, pos)
    in_place = [VMEM] * 6
    row_stat, col_stat = call(
        forward_kernel, [row_shape, shape((16, ROWS), F32)],
        *common, *imgs, txt0, txt1, arrived,
        specs=[SMEM, SMEM, VMEM] + in_place + [anywhere],
    )
    for row_moves, col_move in ((ring_a, pair_z(False)), (ring_b, pair_z(True))):
        row_stat, col_stat = call(
            merge_kernel, [row_shape, shape((16, ROWS), F32)],
            *gathered(row_stat, row_moves), col_stat, shifted(col_stat, col_move),
        )
    tail = shape((EXTRA, WIDTH), BF16)
    row_shift, col_shift, row_tail, col_tail = call(
        shifts_kernel, [shape((16, ROWS), F32), shape((1, 8 * ROWS), F32), tail, tail],
        ids, row_stat, col_stat, shifted(col_stat, other_core),
        specs=[SMEM] + [VMEM] * 3, scratch=[pltpu.VMEM((8, ROWS), F32)],
    )

    sent = shape((QUAD + EXTRA, WIDTH), BF16)
    *dlogits, txt_own, txt_other = call(
        dlogit_kernel, [shape((QUAD, 8 * ROWS), BF16)] * 4 + [sent] * 2,
        *common, row_shift, col_shift, row_tail, *imgs, txt0, txt1,
        specs=[SMEM, SMEM] + [VMEM] * 4 + in_place,
        scratch=[pltpu.VMEM((8 * ROWS, WIDTH), F32)],
    )
    small = [shape((ROWS + EXTRA, WIDTH), BF16)] * 4
    grads = [
        call(
            images_kernel, sent, scale, col_tail, txt0, txt1, d, specs=[SMEM] + [VMEM] * 4
        )
        for d in dlogits
    ]
    txt_parts = call(
        partial_kernel, small, txt_own, shifted(txt_other, other_core)
    )
    txt_parts = scattered(txt_parts, ring_z)
    img_parts = call(
        lambda _, *refs: partial_kernel(*refs), small, txt_parts[0], *scattered(grads, ring_b),
        specs=[anywhere] + [VMEM] * 4,
    )
    img_parts = scattered(img_parts, ring_a)
    whole = shape((ROWS, WIDTH), F32)
    one = shape((1,), F32)
    return pl.pallas_call(
        functools.partial(finish_kernel, 128 * ROWS),
        out_shape=(whole, whole, one, one),
        in_specs=[VMEM] * 10,
        out_specs=(VMEM, VMEM, SMEM, SMEM),
        compiler_params=PARAMS,
    )(images, texts, *img_parts, *txt_parts)


def solution(mesh):
    placed = (P(("row", "col"), None), P(("row", "col"), None), P("row"), P())
    return jax.shard_map(
        on_device,
        mesh=mesh,
        in_specs=placed,
        out_specs=(P(("row", "col"), None), P(("row", "col"), None), P(), P()),
        check_vma=False,
    )
```

```python
import functools

import jax
import jax.numpy as jnp
from jax import lax
from jax.experimental import pallas as pl
from jax.experimental.pallas import tpu as pltpu
from jax.sharding import PartitionSpec as P

ROWS = 128
WIDTH = 512
QUAD = 4 * ROWS
EXTRA = 16
OFFS = (0, 1, 3, 2)
LOG2E = 1.4426950408889634
LN2 = 0.6931471805599453
RC = ("row", "col")
F32 = jnp.float32
BF16 = jnp.bfloat16
VMEM = pl.BlockSpec(memory_space=pltpu.VMEM)
SMEM = pl.BlockSpec(memory_space=pltpu.SMEM)
BUSY = pl.CostEstimate(flops=10**10, bytes_accessed=10**6, transcendentals=0)
PARAMS = pltpu.CompilerParams(vmem_limit_bytes=24 * 1024 * 1024)


def device(z, k, x, y):
    return (z * 2 + k) * 16 + x * 4 + y


def shifted(value, move):
    pairs = []
    for z in range(4):
        for k in range(2):
            for x in range(4):
                for y in range(4):
                    pairs.append((device(z, k, x, y), device(*move(z, k, x, y))))
    return lax.ppermute(value, RC, pairs)


def ring_a(by):
    return lambda z, k, x, y: (z, k, x, (y + by) % 4) if k else (z, k, (x + by) % 4, y)


def ring_b(by):
    return lambda z, k, x, y: (z, k, (x + by) % 4, y) if k else (z, k, x, (y + by) % 4)


def ring_z(by):
    return lambda z, k, x, y: ((z + by) % 4, k, x, y)


def other_core(z, k, x, y):
    return (z, 1 - k, x, y)


def call(kernel, outs, *args, specs=None, cost=None, scratch=()):
    return pl.pallas_call(
        kernel,
        out_shape=outs,
        in_specs=specs or [VMEM] * len(args),
        out_specs=jax.tree.map(lambda o: VMEM, outs),
        scratch_shapes=scratch,
        compiler_params=PARAMS,
        cost_estimate=cost,
    )(*args)


def shape(dims, dtype):
    return jax.ShapeDtypeStruct(dims, dtype)


def unit_rows(values):
    widened = values.astype(F32)
    inverse = lax.rsqrt(jnp.sum(widened * widened, axis=1, keepdims=True) + 1e-06)
    return widened * inverse, inverse


def unit_kernel(raw_ref, *refs):
    refs[-1][...] = unit_rows(raw_ref[...])[0].astype(BF16)


def after_kernel(*refs):
    refs[-1][...] = jnp.zeros_like(refs[-1])


def places(ids_ref):
    row, col = ids_ref[0], ids_ref[1]
    z, k, x, y = row // 2, row % 2, col // 4, col % 4
    pos_a = jnp.where(k == 0, x, y)
    pos_b = jnp.where(k == 0, y, x)

    def col_of(q, a):
        in_b = (pos_b + 4 - OFFS[q]) % 4
        in_a = (pos_a + 4 - OFFS[a]) % 4
        return jnp.where(k == 0, in_a * 4 + in_b, in_b * 4 + in_a)

    def row_of(j, t):
        return (z + 4 - OFFS[t]) % 4 * 2 + (k if j == 0 else 1 - k)

    return col_of, row_of


def to_lanes(column):
    return jnp.transpose(jnp.broadcast_to(column, (ROWS, ROWS)))[0:1, :]


def logits2(rows, t0, t1, scale2):
    parts = [
        lax.dot_general(rows, t[...], (((1,), (1,)), ((), ())), preferred_element_type=F32)
        for t in (t0, t1)
    ]
    return jnp.concatenate(parts, axis=1) * scale2


CHUNK = 256


def forward_kernel(last, places_of, ids_ref, scale_ref, pos_ref, i0, i1, t0, t1, *refs):
    scale2 = scale_ref[0] * LOG2E
    col_of, row_of = places(ids_ref)
    lanes = lax.broadcasted_iota(jnp.int32, (CHUNK, 8 * ROWS), 1)
    if last:
        row_in, state_in, row_out, col_out = refs
        row_out[...] = row_in[...]
        col_high, col_total, col_weighted, picked = (state_in[i : i + 1, :] for i in range(4))
    else:
        _, row_out, state_out = refs
        col_high = jnp.full((1, 8 * ROWS), -jnp.inf, F32)
        col_total = col_weighted = picked = jnp.zeros((1, 8 * ROWS), F32)
    for q, rows_ref in zip(places_of, (i0, i1)):
        for h in range(QUAD // CHUNK):
            logits = logits2(rows_ref[h * CHUNK : (h + 1) * CHUNK, :], t0, t1, scale2)
            high = jnp.max(logits, axis=1, keepdims=True)
            weights = jnp.exp2(logits - high)
            total = jnp.sum(weights, axis=1, keepdims=True)
            mean = jnp.sum(weights * logits, axis=1, keepdims=True) / total
            lse = high + jnp.log2(total)
            pos = []
            for b in range(CHUNK // ROWS):
                place = col_of(q, h * (CHUNK // ROWS) + b)
                row_out[pl.ds(place, 1), :] = to_lanes(lse[b * ROWS : (b + 1) * ROWS])
                row_out[pl.ds(16 + place, 1), :] = to_lanes(mean[b * ROWS : (b + 1) * ROWS])
                pos.append(pos_ref[pl.ds(pl.multiple_of(place * ROWS, ROWS), ROWS), :])
            pos = jnp.concatenate(pos, axis=0)
            pos = jnp.concatenate([pos] * 8, axis=1)
            picked += jnp.sum(jnp.where(pos == lanes, logits, 0.0), axis=0, keepdims=True)
            old = col_high
            col_high = jnp.maximum(old, jnp.max(logits, axis=0, keepdims=True))
            rescale = jnp.exp2(old - col_high)
            weights = jnp.exp2(logits - col_high)
            col_total = col_total * rescale + jnp.sum(weights, axis=0, keepdims=True)
            col_weighted = col_weighted * rescale + jnp.sum(weights * logits, axis=0, keepdims=True)
    if not last:
        for i, value in enumerate((col_high, col_total, col_weighted, picked)):
            state_out[i : i + 1, :] = value
        return
    row_out[32:40, :] = jnp.broadcast_to(jnp.sum(picked, axis=1, keepdims=True), (8, ROWS))
    col_lse = col_high + jnp.log2(col_total)
    col_mean = col_weighted / col_total
    for j in range(2):
        for t in range(4):
            at = (j * 4 + t) * ROWS
            place = row_of(j, t)
            col_out[pl.ds(place, 1), :] = col_lse[:, at : at + ROWS]
            col_out[pl.ds(8 + place, 1), :] = col_mean[:, at : at + ROWS]


def merged(parts, count):
    lse = [p[0:count, :] for p in parts]
    high = functools.reduce(jnp.maximum, lse)
    weights = [jnp.exp2(p - high) for p in lse]
    total = sum(weights)
    mean = sum(w * p[count : 2 * count, :] for w, p in zip(weights, parts)) / total
    return high + jnp.log2(total), mean


def merge_kernel(r0, r1, r2, r3, c0, c1, row_out, col_out):
    refs = (r0, r1, r2, r3)
    row_out[0:16, :], row_out[16:32, :] = merged(refs, 16)
    row_out[32:40, :] = sum(r[32:40, :] for r in refs)
    col_out[0:8, :], col_out[8:16, :] = merged((c0, c1), 8)


def in_parts(first, second):
    lane = lax.broadcasted_iota(jnp.int32, (EXTRA, WIDTH), 1)
    part = lax.broadcasted_iota(jnp.int32, (EXTRA, WIDTH), 0)
    value = jnp.where(lane == 0, first, jnp.where(lane == 1, second, 0.0))
    high = value.astype(BF16)
    rest = value - high.astype(F32)
    mid = rest.astype(BF16)
    low = (rest - mid.astype(F32)).astype(BF16)
    zero = jnp.zeros((EXTRA, WIDTH), F32)
    out = jnp.where(part == 0, high.astype(F32), zero)
    out = jnp.where(part == 1, mid.astype(F32), out)
    return jnp.where(part == 2, low.astype(F32), out).astype(BF16)


def shifts_kernel(ids_ref, row_ref, c0, c1, row_shift, columns, row_tail, col_tail, col_shift):
    _, row_of = places(ids_ref)
    row_lse, row_mean = row_ref[0:16, :], row_ref[16:32, :]
    col_lse, col_mean = merged((c0, c1), 8)
    picked = row_ref[32:33, 0:1]
    row_shift[...] = row_lse + 1.0
    col_shift[...] = col_lse + 1.0
    columns[...] = jnp.concatenate(
        [col_shift[pl.ds(row_of(j, t), 1), :] for j in range(2) for t in range(4)], axis=1
    )
    row_tail[...] = in_parts(
        (jnp.sum(row_lse, keepdims=True) - 2.0 * picked) * LN2,
        (jnp.sum(row_mean, keepdims=True) - 2.0 * picked) * LN2,
    )
    col_tail[...] = in_parts(
        jnp.sum(col_lse, keepdims=True) * LN2, jnp.sum(col_mean, keepdims=True) * LN2
    )


def images_grad(scale_ref, col_tail, t0, t1, d_ref, g_ref):
    product = jnp.dot(d_ref[:, :QUAD], t0[...], preferred_element_type=F32)
    product += jnp.dot(d_ref[:, QUAD:], t1[...], preferred_element_type=F32)
    g_ref[0:QUAD, :] = (scale_ref[0] * product).astype(BF16)
    g_ref[QUAD : QUAD + EXTRA, :] = col_tail[...]


def dlogit_kernel(
    ids_ref, scale_ref, pos_ref, row_shift, col_shift, i0, i1, i2, i3, t0, t1, d0, d1, d2, d3
):
    scale2 = scale_ref[0] * LOG2E
    col_of, row_of = places(ids_ref)
    columns = col_shift[...]
    lanes = lax.broadcasted_iota(jnp.int32, (ROWS, 8 * ROWS), 1)
    for q, (rows_ref, d_ref) in enumerate(zip((i0, i1, i2, i3), (d0, d1, d2, d3))):
        for h in range(QUAD // CHUNK):
            rows = rows_ref[h * CHUNK : (h + 1) * CHUNK, :]
            logits = logits2(rows, t0, t1, scale2)
            pieces = []
            for b in range(CHUNK // ROWS):
                place = col_of(q, h * (CHUNK // ROWS) + b)
                shift = jnp.transpose(jnp.broadcast_to(row_shift[pl.ds(place, 1), :], (ROWS, ROWS)))
                pos = pos_ref[pl.ds(pl.multiple_of(place * ROWS, ROWS), ROWS), :]
                shift = jnp.concatenate([shift] * 8, axis=1)
                pos = jnp.concatenate([pos] * 8, axis=1)
                part = logits[b * ROWS : (b + 1) * ROWS]
                soft = jnp.exp2(part - shift) + jnp.exp2(part - columns)
                pieces.append(jnp.where(pos == lanes, soft - 1.0, soft).astype(BF16))
            d_ref[h * CHUNK : (h + 1) * CHUNK, :] = jnp.concatenate(pieces, axis=0)


def texts_grad_kernel(scale_ref, row_tail, i0, i1, i2, i3, d0, d1, d2, d3, *refs, j):
    out = refs[-1]
    rows = jnp.concatenate([r[...] for r in (i0, i1, i2, i3)], axis=0)
    part = jnp.concatenate([d[:, j * QUAD : (j + 1) * QUAD] for d in (d0, d1, d2, d3)], axis=0)
    update = lax.dot_general(rows, part, (((0,), (0,)), ((), ())), preferred_element_type=F32)
    out[0:QUAD, :] = (scale_ref[0] * jnp.transpose(update)).astype(BF16)
    out[QUAD : QUAD + EXTRA, :] = row_tail[...]


def tail_sum(refs, first):
    total = sum(r[first : first + EXTRA, :].astype(F32) for r in refs)
    total = jnp.sum(total, axis=0, keepdims=True)
    return total[:, 0:1], total[:, 1:2]


def partial_kernel(*refs):
    sources, outs = refs[:-4], refs[-4:]
    tail = in_parts(*tail_sum(sources, QUAD))
    for t, out in enumerate(outs):
        rows = slice(t * ROWS, (t + 1) * ROWS)
        out[0:ROWS, :] = sum(r[rows, :].astype(F32) for r in sources).astype(BF16)
        out[ROWS : ROWS + EXTRA, :] = tail


def finish_kernel(batch, img_ref, txt_ref, a0, a1, a2, a3, b0, b1, b2, b3, img_out, txt_out, loss_out, temp_out):
    for raw, parts, out in ((img_ref, (a0, a1, a2, a3), img_out), (txt_ref, (b0, b1, b2, b3), txt_out)):
        unit, inverse = unit_rows(raw[...])
        grad = sum(p[0:ROWS, :].astype(F32) for p in parts)
        out[...] = inverse * (grad - unit * jnp.sum(unit * grad, axis=1, keepdims=True))
    cols = tail_sum((a0, a1, a2, a3), ROWS)
    rows = tail_sum((b0, b1, b2, b3), ROWS)
    loss_out[0] = jnp.sum(cols[0] + rows[0]) / (2 * batch)
    temp_out[0] = jnp.sum(cols[1] + rows[1]) / (2 * batch)


def gathered(value, moves):
    return [value] + [shifted(value, moves(by)) for by in OFFS[1:]]


def scattered(parts, moves):
    return [parts[0]] + [shifted(p, moves(-by)) for p, by in zip(parts[1:], OFFS[1:])]


def across(place, far):
    return 3 - place if far else place ^ 1


def pair_z(far):
    return lambda z, k, x, y: (across(z, far), k, x, y)


def on_device(images, texts, partner, log_scale):
    row, col = lax.axis_index("row"), lax.axis_index("col")
    ids = jnp.stack([row, col]).astype(jnp.int32)
    scale = jnp.exp(log_scale)
    unit = shape((ROWS, WIDTH), BF16)
    anywhere = pl.BlockSpec(memory_space=pl.ANY)
    anywhere = pl.BlockSpec(memory_space=pl.ANY)
    token = shape((8, ROWS), F32)
    unit_img = call(unit_kernel, unit, images)
    unit_txt = call(unit_kernel, unit, texts, unit_img, specs=[VMEM, anywhere])
    img_own = jnp.concatenate(gathered(unit_img, ring_a), axis=0)
    txt0 = jnp.concatenate(gathered(unit_txt, ring_z), axis=0)
    imgs = gathered(img_own, ring_b)
    txt1 = shifted(txt0, other_core)
    arrived = call(after_kernel, token, imgs[3])

    owner = partner // (16 * ROWS)
    steps = (row // 2 - owner // 2) % 4
    slot = steps ^ (steps // 2)
    core = jnp.where(owner % 2 == row % 2, 0, 1)
    pos = (core * 4 + slot) * ROWS + partner % ROWS
    pos = jnp.where(partner // ROWS % 16 == col, pos, -1)
    pos = jnp.broadcast_to(pos[:, None], (16 * ROWS, ROWS))

    row_shape = shape((40, ROWS), F32)
    common = (ids, scale, pos)
    stats = call(
        functools.partial(forward_kernel, False, (0, 3)), [row_shape, shape((8, 8 * ROWS), F32)],
        *common, imgs[0], imgs[3], txt0, txt1, arrived, specs=[SMEM, SMEM] + [VMEM] * 6,
    )
    row_stat, col_stat = call(
        functools.partial(forward_kernel, True, (2, 1)), [row_shape, shape((16, ROWS), F32)],
        *common, imgs[2], imgs[1], txt0, txt1, *stats, specs=[SMEM, SMEM] + [VMEM] * 7,
    )
    for row_moves, col_move in ((ring_a, pair_z(False)), (ring_b, pair_z(True))):
        row_stat, col_stat = call(
            merge_kernel, [row_shape, shape((16, ROWS), F32)],
            *gathered(row_stat, row_moves), col_stat, shifted(col_stat, col_move),
        )
    tail = shape((EXTRA, WIDTH), BF16)
    row_shift, col_shift, row_tail, col_tail = call(
        shifts_kernel, [shape((16, ROWS), F32), shape((1, 8 * ROWS), F32), tail, tail],
        ids, row_stat, col_stat, shifted(col_stat, other_core),
        specs=[SMEM] + [VMEM] * 3, scratch=[pltpu.VMEM((8, ROWS), F32)],
    )

    sent = shape((QUAD + EXTRA, WIDTH), BF16)
    small = [shape((ROWS + EXTRA, WIDTH), BF16)] * 4
    dlogits = call(
        dlogit_kernel, [shape((QUAD, 8 * ROWS), BF16)] * 4,
        *common, row_shift, col_shift, *imgs, txt0, txt1, cost=BUSY, specs=[SMEM, SMEM] + [VMEM] * 9,
    )
    grads = [
        call(images_grad, sent, scale, col_tail, txt0, txt1, d, cost=BUSY, specs=[SMEM] + [VMEM] * 4)
        for d in dlogits
    ]
    texts_args = (scale, row_tail, *imgs, *dlogits)
    txt_other = call(
        functools.partial(texts_grad_kernel, j=1), sent, *texts_args, *grads[1:],
        cost=BUSY, specs=[SMEM] + [VMEM] * 12,
    )
    txt_own = call(
        functools.partial(texts_grad_kernel, j=0), sent, *texts_args, txt_other,
        cost=BUSY, specs=[SMEM] + [VMEM] * 10,
    )
    txt_parts = call(
        partial_kernel, small, txt_own, shifted(txt_other, other_core)
    )
    txt_parts = scattered(txt_parts, ring_z)
    img_parts = call(
        lambda _, *refs: partial_kernel(*refs), small, txt_parts[0], *scattered(grads, ring_b),
        specs=[anywhere] + [VMEM] * 4,
    )
    img_parts = scattered(img_parts, ring_a)
    whole = shape((ROWS, WIDTH), F32)
    one = shape((1,), F32)
    return pl.pallas_call(
        functools.partial(finish_kernel, 128 * ROWS),
        out_shape=(whole, whole, one, one),
        in_specs=[VMEM] * 10,
        out_specs=(VMEM, VMEM, SMEM, SMEM),
        compiler_params=PARAMS,
    )(images, texts, *img_parts, *txt_parts)


def solution(mesh):
    placed = (P(("row", "col"), None), P(("row", "col"), None), P("row"), P())
    return jax.shard_map(
        on_device,
        mesh=mesh,
        in_specs=placed,
        out_specs=(P(("row", "col"), None), P(("row", "col"), None), P(), P()),
        check_vma=False,
    )
```

```python
import functools

import jax
import jax.numpy as jnp
from jax import lax
from jax.experimental import pallas as pl
from jax.experimental.pallas import tpu as pltpu
from jax.sharding import PartitionSpec as P

ROWS = 128
WIDTH = 512
QUAD = 4 * ROWS
EXTRA = 16
OFFS = (0, 1, 3, 2)
LOG2E = 1.4426950408889634
LN2 = 0.6931471805599453
RC = ("row", "col")
F32 = jnp.float32
BF16 = jnp.bfloat16
VMEM = pl.BlockSpec(memory_space=pltpu.VMEM)
SMEM = pl.BlockSpec(memory_space=pltpu.SMEM)
BUSY = pl.CostEstimate(flops=10**10, bytes_accessed=10**6, transcendentals=0)
PARAMS = pltpu.CompilerParams(vmem_limit_bytes=24 * 1024 * 1024)


def device(z, k, x, y):
    return (z * 2 + k) * 16 + x * 4 + y


def shifted(value, move):
    pairs = []
    for z in range(4):
        for k in range(2):
            for x in range(4):
                for y in range(4):
                    pairs.append((device(z, k, x, y), device(*move(z, k, x, y))))
    return lax.ppermute(value, RC, pairs)


def ring_a(by):
    return lambda z, k, x, y: (z, k, x, (y + by) % 4) if k else (z, k, (x + by) % 4, y)


def ring_b(by):
    return lambda z, k, x, y: (z, k, (x + by) % 4, y) if k else (z, k, x, (y + by) % 4)


def ring_z(by):
    return lambda z, k, x, y: ((z + by) % 4, k, x, y)


def other_core(z, k, x, y):
    return (z, 1 - k, x, y)


def call(kernel, outs, *args, specs=None, cost=None, scratch=()):
    return pl.pallas_call(
        kernel,
        out_shape=outs,
        in_specs=specs or [VMEM] * len(args),
        out_specs=jax.tree.map(lambda o: VMEM, outs),
        scratch_shapes=scratch,
        compiler_params=PARAMS,
        cost_estimate=cost,
    )(*args)


def shape(dims, dtype):
    return jax.ShapeDtypeStruct(dims, dtype)


def unit_rows(values):
    widened = values.astype(F32)
    inverse = lax.rsqrt(jnp.sum(widened * widened, axis=1, keepdims=True) + 1e-06)
    return widened * inverse, inverse


def unit_kernel(raw_ref, *refs):
    refs[-1][...] = unit_rows(raw_ref[...])[0].astype(BF16)


def after_kernel(*refs):
    refs[-1][...] = jnp.zeros_like(refs[-1])


def places(ids_ref):
    row, col = ids_ref[0], ids_ref[1]
    z, k, x, y = row // 2, row % 2, col // 4, col % 4
    pos_a = jnp.where(k == 0, x, y)
    pos_b = jnp.where(k == 0, y, x)

    def col_of(q, a):
        in_b = (pos_b + 4 - OFFS[q]) % 4
        in_a = (pos_a + 4 - OFFS[a]) % 4
        return jnp.where(k == 0, in_a * 4 + in_b, in_b * 4 + in_a)

    def row_of(j, t):
        return (z + 4 - OFFS[t]) % 4 * 2 + (k if j == 0 else 1 - k)

    return col_of, row_of


def to_lanes(column):
    return jnp.transpose(jnp.broadcast_to(column, (ROWS, ROWS)))[0:1, :]


def logits2(rows, t0, t1, scale2):
    parts = [
        lax.dot_general(rows, t[...], (((1,), (1,)), ((), ())), preferred_element_type=F32)
        for t in (t0, t1)
    ]
    return jnp.concatenate(parts, axis=1) * scale2


CHUNK = 256


def either_way(scale_ref, part):
    bounded = scale_ref[0] * (LOG2E * 1.01) <= 100.0
    pl.when(bounded)(functools.partial(part, True))
    pl.when(jnp.logical_not(bounded))(functools.partial(part, False))


def forward_kernel(last, places_of, ids_ref, scale_ref, *refs):
    either_way(
        scale_ref, lambda bounded: forward_part(bounded, last, places_of, ids_ref, scale_ref, *refs)
    )


def lane_sums(values):
    part = sum(values[:, c * ROWS : (c + 1) * ROWS] for c in range(8))
    return jnp.sum(jnp.transpose(part), axis=0, keepdims=True)


def forward_part(bounded, last, places_of, ids_ref, scale_ref, pos_ref, i0, i1, t0, t1, *refs):
    scale2 = scale_ref[0] * LOG2E
    col_of, row_of = places(ids_ref)
    lanes = lax.broadcasted_iota(jnp.int32, (1, 8 * ROWS), 1)
    if last:
        row_in, state_in, row_out, col_out = refs
        row_out[...] = row_in[...]
        col_high, col_total, col_weighted, picked = (state_in[i : i + 1, :] for i in range(4))
    else:
        _, row_out, state_out = refs
        col_high = jnp.full((1, 8 * ROWS), 0.0 if bounded else -jnp.inf, F32)
        col_total = col_weighted = picked = jnp.zeros((1, 8 * ROWS), F32)
    for q, rows_ref in zip(places_of, (i0, i1)):
        for h in range(QUAD // CHUNK):
            logits = logits2(rows_ref[h * CHUNK : (h + 1) * CHUNK, :], t0, t1, scale2)
            if bounded:
                weights = jnp.exp2(logits)
                weighted = weights * logits
                col_total += jnp.sum(weights, axis=0, keepdims=True)
                col_weighted += jnp.sum(weighted, axis=0, keepdims=True)
            else:
                high = jnp.max(logits, axis=1, keepdims=True)
                weights = jnp.exp2(logits - high)
                total = jnp.sum(weights, axis=1, keepdims=True)
                mean = jnp.sum(weights * logits, axis=1, keepdims=True) / total
                lse = high + jnp.log2(total)
                old = col_high
                col_high = jnp.maximum(old, jnp.max(logits, axis=0, keepdims=True))
                rescale = jnp.exp2(old - col_high)
                weights = jnp.exp2(logits - col_high)
                col_total = col_total * rescale + jnp.sum(weights, axis=0, keepdims=True)
                col_weighted = col_weighted * rescale + jnp.sum(
                    weights * logits, axis=0, keepdims=True
                )
            pos = []
            for b in range(CHUNK // ROWS):
                place = col_of(q, h * (CHUNK // ROWS) + b)
                block = slice(b * ROWS, (b + 1) * ROWS)
                if bounded:
                    total = lane_sums(weights[block])
                    row_out[pl.ds(place, 1), :] = jnp.log2(total)
                    row_out[pl.ds(16 + place, 1), :] = lane_sums(weighted[block]) / total
                else:
                    row_out[pl.ds(place, 1), :] = to_lanes(lse[block])
                    row_out[pl.ds(16 + place, 1), :] = to_lanes(mean[block])
                pos.append(pos_ref[pl.ds(pl.multiple_of(place * ROWS, ROWS), ROWS), :])
            pos = jnp.concatenate(pos, axis=0)
            pos = jnp.concatenate([pos] * 8, axis=1)
            picked += jnp.sum(jnp.where(pos == lanes, logits, 0.0), axis=0, keepdims=True)
    if not last:
        for i, value in enumerate((col_high, col_total, col_weighted, picked)):
            state_out[i : i + 1, :] = value
        return
    row_out[32:40, :] = jnp.broadcast_to(jnp.sum(picked, axis=1, keepdims=True), (8, ROWS))
    col_lse = col_high + jnp.log2(col_total)
    col_mean = col_weighted / col_total
    for j in range(2):
        for t in range(4):
            at = (j * 4 + t) * ROWS
            place = row_of(j, t)
            col_out[pl.ds(place, 1), :] = col_lse[:, at : at + ROWS]
            col_out[pl.ds(8 + place, 1), :] = col_mean[:, at : at + ROWS]


def merged(parts, count):
    lse = [p[0:count, :] for p in parts]
    high = functools.reduce(jnp.maximum, lse)
    weights = [jnp.exp2(p - high) for p in lse]
    total = sum(weights)
    mean = sum(w * p[count : 2 * count, :] for w, p in zip(weights, parts)) / total
    return high + jnp.log2(total), mean


def merge_kernel(*refs):
    *refs, c0, c1, row_out, col_out = refs
    row_out[0:16, :], row_out[16:32, :] = merged(refs, 16)
    row_out[32:40, :] = sum(r[32:40, :] for r in refs)
    col_out[0:8, :], col_out[8:16, :] = merged((c0, c1), 8)


def in_parts(first, second):
    lane = lax.broadcasted_iota(jnp.int32, (EXTRA, WIDTH), 1)
    part = lax.broadcasted_iota(jnp.int32, (EXTRA, WIDTH), 0)
    value = jnp.where(lane == 0, first, jnp.where(lane == 1, second, 0.0))
    high = value.astype(BF16)
    rest = value - high.astype(F32)
    mid = rest.astype(BF16)
    low = (rest - mid.astype(F32)).astype(BF16)
    zero = jnp.zeros((EXTRA, WIDTH), F32)
    out = jnp.where(part == 0, high.astype(F32), zero)
    out = jnp.where(part == 1, mid.astype(F32), out)
    return jnp.where(part == 2, low.astype(F32), out).astype(BF16)


def shifts_kernel(ids_ref, r0, r1, c0, c1, row_shift, columns, row_tail, col_tail, col_shift):
    _, row_of = places(ids_ref)
    row_lse, row_mean = merged((r0, r1), 16)
    col_lse, col_mean = merged((c0, c1), 8)
    picked = r0[32:33, 0:1] + r1[32:33, 0:1]
    row_shift[...] = row_lse + 1.0
    col_shift[...] = col_lse + 1.0
    columns[...] = jnp.concatenate(
        [col_shift[pl.ds(row_of(j, t), 1), :] for j in range(2) for t in range(4)], axis=1
    )
    row_tail[...] = in_parts(
        (jnp.sum(row_lse, keepdims=True) - 2.0 * picked) * LN2,
        (jnp.sum(row_mean, keepdims=True) - 2.0 * picked) * LN2,
    )
    col_tail[...] = in_parts(
        jnp.sum(col_lse, keepdims=True) * LN2, jnp.sum(col_mean, keepdims=True) * LN2
    )


def images_grad(scale_ref, col_tail, t0, t1, d_ref, g_ref):
    product = jnp.dot(d_ref[:, :QUAD], t0[...], preferred_element_type=F32)
    product += jnp.dot(d_ref[:, QUAD:], t1[...], preferred_element_type=F32)
    g_ref[0:QUAD, :] = (scale_ref[0] * product).astype(BF16)
    g_ref[QUAD : QUAD + EXTRA, :] = col_tail[...]


def dlogit_kernel(ids_ref, scale_ref, *refs):
    either_way(scale_ref, lambda bounded: dlogit_part(bounded, ids_ref, scale_ref, *refs))


def dlogit_part(
    bounded, ids_ref, scale_ref, pos_ref, row_shift, col_shift, i0, i1, i2, i3, t0, t1,
    d0, d1, d2, d3,
):
    scale2 = scale_ref[0] * LOG2E
    col_of, row_of = places(ids_ref)
    columns = jnp.exp2(-col_shift[...]) if bounded else col_shift[...]
    lanes = lax.broadcasted_iota(jnp.int32, (1, 8 * ROWS), 1)
    for q, (rows_ref, d_ref) in enumerate(zip((i0, i1, i2, i3), (d0, d1, d2, d3))):
        for h in range(QUAD // CHUNK):
            rows = rows_ref[h * CHUNK : (h + 1) * CHUNK, :]
            logits = logits2(rows, t0, t1, scale2)
            pieces = []
            for b in range(CHUNK // ROWS):
                place = col_of(q, h * (CHUNK // ROWS) + b)
                shift = row_shift[pl.ds(place, 1), :]
                shift = jnp.exp2(-shift) if bounded else shift
                shift = jnp.transpose(jnp.broadcast_to(shift, (ROWS, ROWS)))
                pos = pos_ref[pl.ds(pl.multiple_of(place * ROWS, ROWS), ROWS), :]
                shift = jnp.concatenate([shift] * 8, axis=1)
                pos = jnp.concatenate([pos] * 8, axis=1)
                part = logits[b * ROWS : (b + 1) * ROWS]
                if bounded:
                    soft = jnp.exp2(part) * (shift + columns)
                else:
                    soft = jnp.exp2(part - shift) + jnp.exp2(part - columns)
                pieces.append(jnp.where(pos == lanes, soft - 1.0, soft).astype(BF16))
            d_ref[h * CHUNK : (h + 1) * CHUNK, :] = jnp.concatenate(pieces, axis=0)


def texts_grad_kernel(scale_ref, row_tail, i0, i1, i2, i3, d0, d1, d2, d3, *refs, j):
    out = refs[-1]
    rows = jnp.concatenate([r[...] for r in (i0, i1, i2, i3)], axis=0)
    part = jnp.concatenate([d[:, j * QUAD : (j + 1) * QUAD] for d in (d0, d1, d2, d3)], axis=0)
    update = lax.dot_general(rows, part, (((0,), (0,)), ((), ())), preferred_element_type=F32)
    out[0:QUAD, :] = (scale_ref[0] * jnp.transpose(update)).astype(BF16)
    out[QUAD : QUAD + EXTRA, :] = row_tail[...]


def tail_sum(refs, first):
    total = sum(r[first : first + EXTRA, :].astype(F32) for r in refs)
    total = jnp.sum(total, axis=0, keepdims=True)
    return total[:, 0:1], total[:, 1:2]


def partial_kernel(*refs):
    sources, outs = refs[:-4], refs[-4:]
    tail = in_parts(*tail_sum(sources, QUAD))
    for t, out in enumerate(outs):
        rows = slice(t * ROWS, (t + 1) * ROWS)
        out[0:ROWS, :] = sum(r[rows, :].astype(F32) for r in sources).astype(BF16)
        out[ROWS : ROWS + EXTRA, :] = tail


def finish_kernel(batch, img_ref, txt_ref, a0, a1, a2, a3, b0, b1, b2, b3, img_out, txt_out, loss_out, temp_out):
    for raw, parts, out in ((img_ref, (a0, a1, a2, a3), img_out), (txt_ref, (b0, b1, b2, b3), txt_out)):
        unit, inverse = unit_rows(raw[...])
        grad = sum(p[0:ROWS, :].astype(F32) for p in parts)
        out[...] = inverse * (grad - unit * jnp.sum(unit * grad, axis=1, keepdims=True))
    cols = tail_sum((a0, a1, a2, a3), ROWS)
    rows = tail_sum((b0, b1, b2, b3), ROWS)
    loss_out[0] = jnp.sum(cols[0] + rows[0]) / (2 * batch)
    temp_out[0] = jnp.sum(cols[1] + rows[1]) / (2 * batch)


def gathered(value, moves):
    return [value] + [shifted(value, moves(by)) for by in OFFS[1:]]


def scattered(parts, moves):
    return [parts[0]] + [shifted(p, moves(-by)) for p, by in zip(parts[1:], OFFS[1:])]


def across(place, far):
    return 3 - place if far else place ^ 1


def pair_b(far):
    return lambda z, k, x, y: (z, k, across(x, far), y) if k else (z, k, x, across(y, far))


def pair_z(far):
    return lambda z, k, x, y: (across(z, far), k, x, y)


def on_device(images, texts, partner, log_scale):
    row, col = lax.axis_index("row"), lax.axis_index("col")
    ids = jnp.stack([row, col]).astype(jnp.int32)
    scale = jnp.exp(log_scale)
    unit = shape((ROWS, WIDTH), BF16)
    anywhere = pl.BlockSpec(memory_space=pl.ANY)
    anywhere = pl.BlockSpec(memory_space=pl.ANY)
    token = shape((8, ROWS), F32)
    unit_img = call(unit_kernel, unit, images)
    unit_txt = call(unit_kernel, unit, texts, unit_img, specs=[VMEM, anywhere])
    img_own = jnp.concatenate(gathered(unit_img, ring_a), axis=0)
    txt0 = jnp.concatenate(gathered(unit_txt, ring_z), axis=0)
    imgs = gathered(img_own, ring_b)
    txt1 = shifted(txt0, other_core)
    arrived = call(after_kernel, token, imgs[3])

    owner = partner // (16 * ROWS)
    steps = (row // 2 - owner // 2) % 4
    slot = steps ^ (steps // 2)
    core = jnp.where(owner % 2 == row % 2, 0, 1)
    pos = (core * 4 + slot) * ROWS + partner % ROWS
    pos = jnp.where(partner // ROWS % 16 == col, pos, -1)
    pos = jnp.broadcast_to(pos[:, None], (16 * ROWS, ROWS))

    row_shape = shape((40, ROWS), F32)
    common = (ids, scale, pos)
    stats = call(
        functools.partial(forward_kernel, False, (0, 3)), [row_shape, shape((8, 8 * ROWS), F32)],
        *common, imgs[0], imgs[3], txt0, txt1, arrived, specs=[SMEM, SMEM] + [VMEM] * 6,
    )
    row_stat, col_stat = call(
        functools.partial(forward_kernel, True, (2, 1)), [row_shape, shape((16, ROWS), F32)],
        *common, imgs[2], imgs[1], txt0, txt1, *stats, specs=[SMEM, SMEM] + [VMEM] * 7,
    )
    col_shape = shape((16, ROWS), F32)
    row_stat, col_stat = call(
        merge_kernel, [row_shape, col_shape],
        *gathered(row_stat, ring_a), col_stat, shifted(col_stat, other_core),
    )
    row_stat, col_stat = call(
        merge_kernel, [row_shape, col_shape],
        row_stat, shifted(row_stat, pair_b(False)), col_stat, shifted(col_stat, pair_z(False)),
    )
    tail = shape((EXTRA, WIDTH), BF16)
    row_shift, col_shift, row_tail, col_tail = call(
        shifts_kernel, [shape((16, ROWS), F32), shape((1, 8 * ROWS), F32), tail, tail],
        ids, row_stat, shifted(row_stat, pair_b(True)), col_stat, shifted(col_stat, pair_z(True)),
        specs=[SMEM] + [VMEM] * 4, scratch=[pltpu.VMEM((8, ROWS), F32)],
    )

    sent = shape((QUAD + EXTRA, WIDTH), BF16)
    small = [shape((ROWS + EXTRA, WIDTH), BF16)] * 4
    dlogits = call(
        dlogit_kernel, [shape((QUAD, 8 * ROWS), BF16)] * 4,
        *common, row_shift, col_shift, *imgs, txt0, txt1, cost=BUSY, specs=[SMEM, SMEM] + [VMEM] * 9,
    )
    grads = [
        call(images_grad, sent, scale, col_tail, txt0, txt1, d, cost=BUSY, specs=[SMEM] + [VMEM] * 4)
        for d in dlogits
    ]
    texts_args = (scale, row_tail, *imgs, *dlogits)
    txt_other = call(
        functools.partial(texts_grad_kernel, j=1), sent, *texts_args, *grads[1:],
        cost=BUSY, specs=[SMEM] + [VMEM] * 12,
    )
    txt_own = call(
        functools.partial(texts_grad_kernel, j=0), sent, *texts_args, txt_other,
        cost=BUSY, specs=[SMEM] + [VMEM] * 10,
    )
    txt_parts = call(
        partial_kernel, small, txt_own, shifted(txt_other, other_core)
    )
    txt_parts = scattered(txt_parts, ring_z)
    img_parts = call(
        lambda _, *refs: partial_kernel(*refs), small, txt_parts[0], *scattered(grads, ring_b),
        specs=[anywhere] + [VMEM] * 4,
    )
    img_parts = scattered(img_parts, ring_a)
    whole = shape((ROWS, WIDTH), F32)
    one = shape((1,), F32)
    return pl.pallas_call(
        functools.partial(finish_kernel, 128 * ROWS),
        out_shape=(whole, whole, one, one),
        in_specs=[VMEM] * 10,
        out_specs=(VMEM, VMEM, SMEM, SMEM),
        compiler_params=PARAMS,
    )(images, texts, *img_parts, *txt_parts)


def solution(mesh):
    placed = (P(("row", "col"), None), P(("row", "col"), None), P("row"), P())
    return jax.shard_map(
        on_device,
        mesh=mesh,
        in_specs=placed,
        out_specs=(P(("row", "col"), None), P(("row", "col"), None), P(), P()),
        check_vma=False,
    )
```

```python
import functools

import jax
import jax.numpy as jnp
from jax import lax
from jax.experimental import pallas as pl
from jax.experimental.pallas import tpu as pltpu
from jax.sharding import PartitionSpec as P

ROWS = 128
WIDTH = 512
QUAD = 4 * ROWS
EXTRA = 16
OFFS = (0, 1, 3, 2)
LOG2E = 1.4426950408889634
LN2 = 0.6931471805599453
RC = ("row", "col")
F32 = jnp.float32
BF16 = jnp.bfloat16
VMEM = pl.BlockSpec(memory_space=pltpu.VMEM)
SMEM = pl.BlockSpec(memory_space=pltpu.SMEM)
BUSY = pl.CostEstimate(flops=10**10, bytes_accessed=10**6, transcendentals=0)
PARAMS = pltpu.CompilerParams(vmem_limit_bytes=12 * 1024 * 1024)


def device(z, k, x, y):
    return (z * 2 + k) * 16 + x * 4 + y


def shifted(value, move):
    pairs = []
    for z in range(4):
        for k in range(2):
            for x in range(4):
                for y in range(4):
                    pairs.append((device(z, k, x, y), device(*move(z, k, x, y))))
    return lax.ppermute(value, RC, pairs)


def ring_a(by):
    return lambda z, k, x, y: (z, k, x, (y + by) % 4) if k else (z, k, (x + by) % 4, y)


def ring_b(by):
    return lambda z, k, x, y: (z, k, (x + by) % 4, y) if k else (z, k, x, (y + by) % 4)


def ring_z(by):
    return lambda z, k, x, y: ((z + by) % 4, k, x, y)


def other_core(z, k, x, y):
    return (z, 1 - k, x, y)


def call(kernel, outs, *args, specs=None, cost=None, scratch=()):
    return pl.pallas_call(
        kernel,
        out_shape=outs,
        in_specs=specs or [VMEM] * len(args),
        out_specs=jax.tree.map(lambda o: VMEM, outs),
        scratch_shapes=scratch,
        compiler_params=PARAMS,
        cost_estimate=cost,
    )(*args)


def shape(dims, dtype):
    return jax.ShapeDtypeStruct(dims, dtype)


def unit_rows(values):
    widened = values.astype(F32)
    inverse = lax.rsqrt(jnp.sum(widened * widened, axis=1, keepdims=True) + 1e-06)
    return widened * inverse, inverse


def unit_kernel(raw_ref, *refs):
    refs[-1][...] = unit_rows(raw_ref[...])[0].astype(BF16)


def after_kernel(*refs):
    refs[-1][...] = jnp.zeros_like(refs[-1])


def places(ids_ref):
    row, col = ids_ref[0], ids_ref[1]
    z, k, x, y = row // 2, row % 2, col // 4, col % 4
    pos_a = jnp.where(k == 0, x, y)
    pos_b = jnp.where(k == 0, y, x)

    def col_of(q, a):
        in_b = (pos_b + 4 - OFFS[q]) % 4
        in_a = (pos_a + 4 - OFFS[a]) % 4
        return jnp.where(k == 0, in_a * 4 + in_b, in_b * 4 + in_a)

    def row_of(j, t):
        return (z + 4 - OFFS[t]) % 4 * 2 + (k if j == 0 else 1 - k)

    return col_of, row_of


def to_lanes(column):
    return jnp.transpose(jnp.broadcast_to(column, (ROWS, ROWS)))[0:1, :]


def logits2(rows, t0, t1, scale2):
    parts = [
        lax.dot_general(rows, t[...], (((1,), (1,)), ((), ())), preferred_element_type=F32)
        for t in (t0, t1)
    ]
    return jnp.concatenate(parts, axis=1) * scale2


CHUNK = 256


def either_way(scale_ref, part):
    bounded = scale_ref[0] * (LOG2E * 1.01) <= 100.0
    pl.when(bounded)(functools.partial(part, True))
    pl.when(jnp.logical_not(bounded))(functools.partial(part, False))


def forward_kernel(last, places_of, ids_ref, scale_ref, *refs):
    either_way(
        scale_ref, lambda bounded: forward_part(bounded, last, places_of, ids_ref, scale_ref, *refs)
    )


def lane_sums(values):
    part = sum(values[:, c * ROWS : (c + 1) * ROWS] for c in range(8))
    return jnp.sum(jnp.transpose(part), axis=0, keepdims=True)


def forward_part(bounded, last, places_of, ids_ref, scale_ref, pos_ref, i0, i1, t0, t1, *refs):
    scale2 = scale_ref[0] * LOG2E
    col_of, row_of = places(ids_ref)
    lanes = lax.broadcasted_iota(jnp.int32, (1, 8 * ROWS), 1)
    if last:
        row_in, state_in, row_out, col_out, *kept = refs
        row_out[...] = row_in[...]
        col_high, col_total, col_weighted, picked = (state_in[i : i + 1, :] for i in range(4))
    else:
        _, row_out, state_out, *kept = refs
        col_high = jnp.full((1, 8 * ROWS), 0.0 if bounded else -jnp.inf, F32)
        col_total = col_weighted = picked = jnp.zeros((1, 8 * ROWS), F32)
    for q, rows_ref, kept_ref in zip(places_of, (i0, i1), kept):
        for h in range(QUAD // CHUNK):
            logits = logits2(rows_ref[h * CHUNK : (h + 1) * CHUNK, :], t0, t1, scale2)
            if bounded:
                weights = jnp.exp2(logits)
                kept_ref[h * CHUNK : (h + 1) * CHUNK, :] = weights
                weighted = weights * logits
                col_total += jnp.sum(weights, axis=0, keepdims=True)
                col_weighted += jnp.sum(weighted, axis=0, keepdims=True)
            else:
                kept_ref[h * CHUNK : (h + 1) * CHUNK, :] = logits
                high = jnp.max(logits, axis=1, keepdims=True)
                weights = jnp.exp2(logits - high)
                total = jnp.sum(weights, axis=1, keepdims=True)
                mean = jnp.sum(weights * logits, axis=1, keepdims=True) / total
                lse = high + jnp.log2(total)
                old = col_high
                col_high = jnp.maximum(old, jnp.max(logits, axis=0, keepdims=True))
                rescale = jnp.exp2(old - col_high)
                weights = jnp.exp2(logits - col_high)
                col_total = col_total * rescale + jnp.sum(weights, axis=0, keepdims=True)
                col_weighted = col_weighted * rescale + jnp.sum(
                    weights * logits, axis=0, keepdims=True
                )
            pos = []
            for b in range(CHUNK // ROWS):
                place = col_of(q, h * (CHUNK // ROWS) + b)
                block = slice(b * ROWS, (b + 1) * ROWS)
                if bounded:
                    total = lane_sums(weights[block])
                    row_out[pl.ds(place, 1), :] = jnp.log2(total)
                    row_out[pl.ds(16 + place, 1), :] = lane_sums(weighted[block]) / total
                else:
                    row_out[pl.ds(place, 1), :] = to_lanes(lse[block])
                    row_out[pl.ds(16 + place, 1), :] = to_lanes(mean[block])
                pos.append(pos_ref[pl.ds(pl.multiple_of(place * ROWS, ROWS), ROWS), :])
            pos = jnp.concatenate(pos, axis=0)
            pos = jnp.concatenate([pos] * 8, axis=1)
            picked += jnp.sum(jnp.where(pos == lanes, logits, 0.0), axis=0, keepdims=True)
    if not last:
        for i, value in enumerate((col_high, col_total, col_weighted, picked)):
            state_out[i : i + 1, :] = value
        return
    row_out[32:40, :] = jnp.broadcast_to(jnp.sum(picked, axis=1, keepdims=True), (8, ROWS))
    col_lse = col_high + jnp.log2(col_total)
    col_mean = col_weighted / col_total
    for j in range(2):
        for t in range(4):
            at = (j * 4 + t) * ROWS
            place = row_of(j, t)
            col_out[pl.ds(place, 1), :] = col_lse[:, at : at + ROWS]
            col_out[pl.ds(8 + place, 1), :] = col_mean[:, at : at + ROWS]


def merged(parts, count):
    lse = [p[0:count, :] for p in parts]
    high = functools.reduce(jnp.maximum, lse)
    weights = [jnp.exp2(p - high) for p in lse]
    total = sum(weights)
    mean = sum(w * p[count : 2 * count, :] for w, p in zip(weights, parts)) / total
    return high + jnp.log2(total), mean


def merge_kernel(*refs):
    *refs, c0, c1, row_out, col_out = refs
    row_out[0:16, :], row_out[16:32, :] = merged(refs, 16)
    row_out[32:40, :] = sum(r[32:40, :] for r in refs)
    col_out[0:8, :], col_out[8:16, :] = merged((c0, c1), 8)


def in_parts(first, second):
    lane = lax.broadcasted_iota(jnp.int32, (EXTRA, WIDTH), 1)
    part = lax.broadcasted_iota(jnp.int32, (EXTRA, WIDTH), 0)
    value = jnp.where(lane == 0, first, jnp.where(lane == 1, second, 0.0))
    high = value.astype(BF16)
    rest = value - high.astype(F32)
    mid = rest.astype(BF16)
    low = (rest - mid.astype(F32)).astype(BF16)
    zero = jnp.zeros((EXTRA, WIDTH), F32)
    out = jnp.where(part == 0, high.astype(F32), zero)
    out = jnp.where(part == 1, mid.astype(F32), out)
    return jnp.where(part == 2, low.astype(F32), out).astype(BF16)


def shifts_kernel(ids_ref, r0, r1, c0, c1, row_shift, columns, row_tail, col_tail, col_shift):
    _, row_of = places(ids_ref)
    row_lse, row_mean = merged((r0, r1), 16)
    col_lse, col_mean = merged((c0, c1), 8)
    picked = r0[32:33, 0:1] + r1[32:33, 0:1]
    row_shift[...] = row_lse + 1.0
    col_shift[...] = col_lse + 1.0
    columns[...] = jnp.concatenate(
        [col_shift[pl.ds(row_of(j, t), 1), :] for j in range(2) for t in range(4)], axis=1
    )
    row_tail[...] = in_parts(
        (jnp.sum(row_lse, keepdims=True) - 2.0 * picked) * LN2,
        (jnp.sum(row_mean, keepdims=True) - 2.0 * picked) * LN2,
    )
    col_tail[...] = in_parts(
        jnp.sum(col_lse, keepdims=True) * LN2, jnp.sum(col_mean, keepdims=True) * LN2
    )


def images_grad(scale_ref, col_tail, t0, t1, d_ref, g_ref):
    product = jnp.dot(d_ref[:, :QUAD], t0[...], preferred_element_type=F32)
    product += jnp.dot(d_ref[:, QUAD:], t1[...], preferred_element_type=F32)
    g_ref[0:QUAD, :] = (scale_ref[0] * product).astype(BF16)
    g_ref[QUAD : QUAD + EXTRA, :] = col_tail[...]


def dlogit_kernel(pieces, ids_ref, scale_ref, *refs):
    either_way(scale_ref, lambda bounded: dlogit_part(bounded, pieces, ids_ref, *refs))


def dlogit_part(bounded, places_of, ids_ref, pos_ref, row_shift, col_shift, *refs):
    count = len(places_of)
    col_of, row_of = places(ids_ref)
    columns = jnp.exp2(-col_shift[...]) if bounded else col_shift[...]
    lanes = lax.broadcasted_iota(jnp.int32, (1, 8 * ROWS), 1)
    for q, kept_ref, d_ref in zip(places_of, refs[:count], refs[count:]):
        for h in range(QUAD // CHUNK):
            kept = kept_ref[h * CHUNK : (h + 1) * CHUNK, :]
            pieces = []
            for b in range(CHUNK // ROWS):
                place = col_of(q, h * (CHUNK // ROWS) + b)
                shift = row_shift[pl.ds(place, 1), :]
                shift = jnp.exp2(-shift) if bounded else shift
                shift = jnp.transpose(jnp.broadcast_to(shift, (ROWS, ROWS)))
                pos = pos_ref[pl.ds(pl.multiple_of(place * ROWS, ROWS), ROWS), :]
                shift = jnp.concatenate([shift] * 8, axis=1)
                pos = jnp.concatenate([pos] * 8, axis=1)
                part = kept[b * ROWS : (b + 1) * ROWS]
                if bounded:
                    soft = part * (shift + columns)
                else:
                    soft = jnp.exp2(part - shift) + jnp.exp2(part - columns)
                pieces.append(jnp.where(pos == lanes, soft - 1.0, soft).astype(BF16))
            d_ref[h * CHUNK : (h + 1) * CHUNK, :] = jnp.concatenate(pieces, axis=0)


def texts_grad_kernel(scale_ref, row_tail, i0, i1, i2, i3, d0, d1, d2, d3, *refs, j):
    out = refs[-1]
    rows = jnp.concatenate([r[...] for r in (i0, i1, i2, i3)], axis=0)
    part = jnp.concatenate([d[:, j * QUAD : (j + 1) * QUAD] for d in (d0, d1, d2, d3)], axis=0)
    update = lax.dot_general(rows, part, (((0,), (0,)), ((), ())), preferred_element_type=F32)
    out[0:QUAD, :] = (scale_ref[0] * jnp.transpose(update)).astype(BF16)
    out[QUAD : QUAD + EXTRA, :] = row_tail[...]


def tail_sum(refs, first):
    total = sum(r[first : first + EXTRA, :].astype(F32) for r in refs)
    total = jnp.sum(total, axis=0, keepdims=True)
    return total[:, 0:1], total[:, 1:2]


def partial_kernel(*refs):
    sources, outs = refs[:-4], refs[-4:]
    tail = in_parts(*tail_sum(sources, QUAD))
    for t, out in enumerate(outs):
        rows = slice(t * ROWS, (t + 1) * ROWS)
        out[0:ROWS, :] = sum(r[rows, :].astype(F32) for r in sources).astype(BF16)
        out[ROWS : ROWS + EXTRA, :] = tail


def finish_kernel(batch, img_ref, txt_ref, a0, a1, a2, a3, b0, b1, b2, b3, img_out, txt_out, loss_out, temp_out):
    for raw, parts, out in ((img_ref, (a0, a1, a2, a3), img_out), (txt_ref, (b0, b1, b2, b3), txt_out)):
        unit, inverse = unit_rows(raw[...])
        grad = sum(p[0:ROWS, :].astype(F32) for p in parts)
        out[...] = inverse * (grad - unit * jnp.sum(unit * grad, axis=1, keepdims=True))
    cols = tail_sum((a0, a1, a2, a3), ROWS)
    rows = tail_sum((b0, b1, b2, b3), ROWS)
    loss_out[0] = jnp.sum(cols[0] + rows[0]) / (2 * batch)
    temp_out[0] = jnp.sum(cols[1] + rows[1]) / (2 * batch)


def gathered(value, moves):
    return [value] + [shifted(value, moves(by)) for by in OFFS[1:]]


def scattered(parts, moves):
    return [parts[0]] + [shifted(p, moves(-by)) for p, by in zip(parts[1:], OFFS[1:])]


def across(place, far):
    return 3 - place if far else place ^ 1


def pair_b(far):
    return lambda z, k, x, y: (z, k, across(x, far), y) if k else (z, k, x, across(y, far))


def pair_z(far):
    return lambda z, k, x, y: (across(z, far), k, x, y)


def on_device(images, texts, partner, log_scale):
    row, col = lax.axis_index("row"), lax.axis_index("col")
    ids = jnp.stack([row, col]).astype(jnp.int32)
    scale = jnp.exp(log_scale)
    unit = shape((ROWS, WIDTH), BF16)
    anywhere = pl.BlockSpec(memory_space=pl.ANY)
    anywhere = pl.BlockSpec(memory_space=pl.ANY)
    token = shape((8, ROWS), F32)
    unit_img = call(unit_kernel, unit, images)
    unit_txt = call(unit_kernel, unit, texts, unit_img, specs=[VMEM, anywhere])
    img_own = jnp.concatenate(gathered(unit_img, ring_a), axis=0)
    txt0 = jnp.concatenate(gathered(unit_txt, ring_z), axis=0)
    imgs = gathered(img_own, ring_b)
    txt1 = shifted(txt0, other_core)
    arrived = call(after_kernel, token, imgs[3])

    owner = partner // (16 * ROWS)
    steps = (row // 2 - owner // 2) % 4
    slot = steps ^ (steps // 2)
    core = jnp.where(owner % 2 == row % 2, 0, 1)
    pos = (core * 4 + slot) * ROWS + partner % ROWS
    pos = jnp.where(partner // ROWS % 16 == col, pos, -1)
    pos = jnp.broadcast_to(pos[:, None], (16 * ROWS, ROWS))

    row_shape = shape((40, ROWS), F32)
    common = (ids, scale, pos)
    kept = shape((QUAD, 8 * ROWS), F32)
    row_stat, state, *near_kept = call(
        functools.partial(forward_kernel, False, (0, 3)),
        [row_shape, shape((8, 8 * ROWS), F32), kept, kept],
        *common, imgs[0], imgs[3], txt0, txt1, arrived, specs=[SMEM, SMEM] + [VMEM] * 6,
    )
    row_stat, col_stat, *far_kept = call(
        functools.partial(forward_kernel, True, (2, 1)),
        [row_shape, shape((16, ROWS), F32), kept, kept],
        *common, imgs[2], imgs[1], txt0, txt1, row_stat, state, specs=[SMEM, SMEM] + [VMEM] * 7,
    )
    kept = (near_kept[0], far_kept[1], far_kept[0], near_kept[1])
    col_shape = shape((16, ROWS), F32)
    row_stat, col_stat = call(
        merge_kernel, [row_shape, col_shape],
        *gathered(row_stat, ring_a), col_stat, shifted(col_stat, other_core),
    )
    row_stat, col_stat = call(
        merge_kernel, [row_shape, col_shape],
        row_stat, shifted(row_stat, pair_b(False)), col_stat, shifted(col_stat, pair_z(False)),
    )
    tail = shape((EXTRA, WIDTH), BF16)
    row_shift, col_shift, row_tail, col_tail = call(
        shifts_kernel, [shape((16, ROWS), F32), shape((1, 8 * ROWS), F32), tail, tail],
        ids, row_stat, shifted(row_stat, pair_b(True)), col_stat, shifted(col_stat, pair_z(True)),
        specs=[SMEM] + [VMEM] * 4, scratch=[pltpu.VMEM((8, ROWS), F32)],
    )

    sent = shape((QUAD + EXTRA, WIDTH), BF16)
    small = [shape((ROWS + EXTRA, WIDTH), BF16)] * 4
    dlogits = {}
    for pieces in ((3,), (2, 1, 0)):
        made = call(
            functools.partial(dlogit_kernel, pieces), [shape((QUAD, 8 * ROWS), BF16)] * len(pieces),
            *common, row_shift, col_shift, *(kept[q] for q in pieces),
            cost=BUSY, specs=[SMEM, SMEM] + [VMEM] * (3 + len(pieces)),
        )
        dlogits.update(zip(pieces, made))
    dlogits = [dlogits[q] for q in range(4)]
    grads = [
        call(images_grad, sent, scale, col_tail, txt0, txt1, d, cost=BUSY, specs=[SMEM] + [VMEM] * 4)
        for d in dlogits
    ]
    texts_args = (scale, row_tail, *imgs, *dlogits)
    txt_other = call(
        functools.partial(texts_grad_kernel, j=1), sent, *texts_args, *grads[1:],
        cost=BUSY, specs=[SMEM] + [VMEM] * 12,
    )
    txt_own = call(
        functools.partial(texts_grad_kernel, j=0), sent, *texts_args, txt_other,
        cost=BUSY, specs=[SMEM] + [VMEM] * 10,
    )
    txt_parts = call(
        partial_kernel, small, txt_own, shifted(txt_other, other_core)
    )
    txt_parts = scattered(txt_parts, ring_z)
    img_parts = call(
        lambda _, *refs: partial_kernel(*refs), small, txt_parts[0], *scattered(grads, ring_b),
        specs=[anywhere] + [VMEM] * 4,
    )
    img_parts = scattered(img_parts, ring_a)
    whole = shape((ROWS, WIDTH), F32)
    one = shape((1,), F32)
    return pl.pallas_call(
        functools.partial(finish_kernel, 128 * ROWS),
        out_shape=(whole, whole, one, one),
        in_specs=[VMEM] * 10,
        out_specs=(VMEM, VMEM, SMEM, SMEM),
        compiler_params=PARAMS,
    )(images, texts, *img_parts, *txt_parts)


def solution(mesh):
    placed = (P(("row", "col"), None), P(("row", "col"), None), P("row"), P())
    return jax.shard_map(
        on_device,
        mesh=mesh,
        in_specs=placed,
        out_specs=(P(("row", "col"), None), P(("row", "col"), None), P(), P()),
        check_vma=False,
    )
```

```python
import functools

import jax
import jax.numpy as jnp
from jax import lax
from jax.experimental import pallas as pl
from jax.experimental.pallas import tpu as pltpu
from jax.sharding import PartitionSpec as P

ROWS = 128
WIDTH = 512
QUAD = 4 * ROWS
EXTRA = 16
OFFS = (0, 1, 3, 2)
LOG2E = 1.4426950408889634
LN2 = 0.6931471805599453
RC = ("row", "col")
F32 = jnp.float32
BF16 = jnp.bfloat16
VMEM = pl.BlockSpec(memory_space=pltpu.VMEM)
SMEM = pl.BlockSpec(memory_space=pltpu.SMEM)
BUSY = pl.CostEstimate(flops=10**10, bytes_accessed=10**6, transcendentals=0)
PARAMS = pltpu.CompilerParams(vmem_limit_bytes=12 * 1024 * 1024)


def device(z, k, x, y):
    return (z * 2 + k) * 16 + x * 4 + y


def shifted(value, move):
    pairs = []
    for z in range(4):
        for k in range(2):
            for x in range(4):
                for y in range(4):
                    pairs.append((device(z, k, x, y), device(*move(z, k, x, y))))
    return lax.ppermute(value, RC, pairs)


def ring_a(by):
    return lambda z, k, x, y: (z, k, x, (y + by) % 4) if k else (z, k, (x + by) % 4, y)


def ring_b(by):
    return lambda z, k, x, y: (z, k, (x + by) % 4, y) if k else (z, k, x, (y + by) % 4)


def ring_z(by):
    return lambda z, k, x, y: ((z + by) % 4, k, x, y)


def other_core(z, k, x, y):
    return (z, 1 - k, x, y)


def call(kernel, outs, *args, specs=None, cost=None, scratch=()):
    return pl.pallas_call(
        kernel,
        out_shape=outs,
        in_specs=specs or [VMEM] * len(args),
        out_specs=jax.tree.map(lambda o: VMEM, outs),
        scratch_shapes=scratch,
        compiler_params=PARAMS,
        cost_estimate=cost,
    )(*args)


def shape(dims, dtype):
    return jax.ShapeDtypeStruct(dims, dtype)


def unit_rows(values):
    widened = values.astype(F32)
    inverse = lax.rsqrt(jnp.sum(widened * widened, axis=1, keepdims=True) + 1e-06)
    return widened * inverse, inverse


def unit_kernel(raw_ref, *refs):
    refs[-1][...] = unit_rows(raw_ref[...])[0].astype(BF16)


def after_kernel(*refs):
    refs[-1][...] = jnp.zeros_like(refs[-1])


def places(ids_ref):
    row, col = ids_ref[0], ids_ref[1]
    z, k, x, y = row // 2, row % 2, col // 4, col % 4
    pos_a = jnp.where(k == 0, x, y)
    pos_b = jnp.where(k == 0, y, x)

    def col_of(q, a):
        in_b = (pos_b + 4 - OFFS[q]) % 4
        in_a = (pos_a + 4 - OFFS[a]) % 4
        return jnp.where(k == 0, in_a * 4 + in_b, in_b * 4 + in_a)

    def row_of(j, t):
        return (z + 4 - OFFS[t]) % 4 * 2 + (k if j == 0 else 1 - k)

    return col_of, row_of


def to_lanes(column):
    return jnp.transpose(jnp.broadcast_to(column, (ROWS, ROWS)))[0:1, :]


def logits2(rows, t0, t1, scale2):
    parts = [
        lax.dot_general(rows, t[...], (((1,), (1,)), ((), ())), preferred_element_type=F32)
        for t in (t0, t1)
    ]
    return jnp.concatenate(parts, axis=1) * scale2


CHUNK = 256


def either_way(scale_ref, part):
    bounded = scale_ref[0] * (LOG2E * 1.01) <= 100.0
    pl.when(bounded)(functools.partial(part, True))
    pl.when(jnp.logical_not(bounded))(functools.partial(part, False))


def forward_kernel(last, places_of, ids_ref, scale_ref, *refs):
    either_way(
        scale_ref, lambda bounded: forward_part(bounded, last, places_of, ids_ref, scale_ref, *refs)
    )


def lane_sums(values):
    part = sum(values[:, c * ROWS : (c + 1) * ROWS] for c in range(8))
    return jnp.sum(jnp.transpose(part), axis=0, keepdims=True)


def forward_part(bounded, last, places_of, ids_ref, scale_ref, pos_ref, i0, i1, t0, t1, *refs):
    scale2 = scale_ref[0] * LOG2E
    col_of, row_of = places(ids_ref)
    lanes = lax.broadcasted_iota(jnp.int32, (1, 8 * ROWS), 1)
    if last:
        row_in, state_in, row_out, col_out, *kept = refs
        row_out[...] = row_in[...]
        col_high, col_total, col_weighted, picked = (state_in[i : i + 1, :] for i in range(4))
    else:
        _, row_out, state_out, *kept = refs
        col_high = jnp.full((1, 8 * ROWS), 0.0 if bounded else -jnp.inf, F32)
        col_total = col_weighted = picked = jnp.zeros((1, 8 * ROWS), F32)
    for q, rows_ref, kept_ref in zip(places_of, (i0, i1), kept):
        for h in range(QUAD // CHUNK):
            logits = logits2(rows_ref[h * CHUNK : (h + 1) * CHUNK, :], t0, t1, scale2)
            if bounded:
                weights = jnp.exp2(logits)
                kept_ref[h * CHUNK : (h + 1) * CHUNK, :] = weights
                weighted = weights * logits
                col_total += jnp.sum(weights, axis=0, keepdims=True)
                col_weighted += jnp.sum(weighted, axis=0, keepdims=True)
            else:
                kept_ref[h * CHUNK : (h + 1) * CHUNK, :] = logits
                high = jnp.max(logits, axis=1, keepdims=True)
                weights = jnp.exp2(logits - high)
                total = jnp.sum(weights, axis=1, keepdims=True)
                mean = jnp.sum(weights * logits, axis=1, keepdims=True) / total
                lse = high + jnp.log2(total)
                old = col_high
                col_high = jnp.maximum(old, jnp.max(logits, axis=0, keepdims=True))
                rescale = jnp.exp2(old - col_high)
                weights = jnp.exp2(logits - col_high)
                col_total = col_total * rescale + jnp.sum(weights, axis=0, keepdims=True)
                col_weighted = col_weighted * rescale + jnp.sum(
                    weights * logits, axis=0, keepdims=True
                )
            pos = []
            for b in range(CHUNK // ROWS):
                place = col_of(q, h * (CHUNK // ROWS) + b)
                block = slice(b * ROWS, (b + 1) * ROWS)
                if bounded:
                    total = lane_sums(weights[block])
                    row_out[pl.ds(place, 1), :] = jnp.log2(total)
                    row_out[pl.ds(16 + place, 1), :] = lane_sums(weighted[block]) / total
                else:
                    row_out[pl.ds(place, 1), :] = to_lanes(lse[block])
                    row_out[pl.ds(16 + place, 1), :] = to_lanes(mean[block])
                pos.append(pos_ref[pl.ds(pl.multiple_of(place * ROWS, ROWS), ROWS), :])
            pos = jnp.concatenate(pos, axis=0)
            pos = jnp.concatenate([pos] * 8, axis=1)
            picked += jnp.sum(jnp.where(pos == lanes, logits, 0.0), axis=0, keepdims=True)
    if not last:
        for i, value in enumerate((col_high, col_total, col_weighted, picked)):
            state_out[i : i + 1, :] = value
        return
    row_out[32:40, :] = jnp.broadcast_to(jnp.sum(picked, axis=1, keepdims=True), (8, ROWS))
    col_out[16:, :] = jnp.zeros_like(col_out[16:, :])
    col_lse = col_high + jnp.log2(col_total)
    col_mean = col_weighted / col_total
    for j in range(2):
        for t in range(4):
            at = (j * 4 + t) * ROWS
            place = row_of(j, t)
            col_out[pl.ds(place, 1), :] = col_lse[:, at : at + ROWS]
            col_out[pl.ds(8 + place, 1), :] = col_mean[:, at : at + ROWS]


def merged(parts, count):
    lse = [p[0:count, :] for p in parts]
    high = functools.reduce(jnp.maximum, lse)
    weights = [jnp.exp2(p - high) for p in lse]
    total = sum(weights)
    mean = sum(w * p[count : 2 * count, :] for w, p in zip(weights, parts)) / total
    return high + jnp.log2(total), mean


def merge_kernel(*refs):
    *refs, c0, c1, row_out, col_out = refs
    row_out[0:16, :], row_out[16:32, :] = merged(refs, 16)
    row_out[32:40, :] = sum(r[32:40, :] for r in refs)
    col_out[0:8, :], col_out[8:16, :] = merged((c0, c1), 8)
    col_out[16:, :] = jnp.zeros_like(col_out[16:, :])


def in_parts(first, second):
    lane = lax.broadcasted_iota(jnp.int32, (EXTRA, WIDTH), 1)
    part = lax.broadcasted_iota(jnp.int32, (EXTRA, WIDTH), 0)
    value = jnp.where(lane == 0, first, jnp.where(lane == 1, second, 0.0))
    high = value.astype(BF16)
    rest = value - high.astype(F32)
    mid = rest.astype(BF16)
    low = (rest - mid.astype(F32)).astype(BF16)
    zero = jnp.zeros((EXTRA, WIDTH), F32)
    out = jnp.where(part == 0, high.astype(F32), zero)
    out = jnp.where(part == 1, mid.astype(F32), out)
    return jnp.where(part == 2, low.astype(F32), out).astype(BF16)


def shifts_kernel(ids_ref, r0, r1, c0, c1, row_shift, columns, row_tail, col_tail, col_shift):
    _, row_of = places(ids_ref)
    row_lse, row_mean = merged((r0, r1), 16)
    col_lse, col_mean = merged((c0, c1), 8)
    picked = r0[32:33, 0:1] + r1[32:33, 0:1]
    row_shift[...] = row_lse + 1.0
    col_shift[...] = col_lse + 1.0
    columns[...] = jnp.concatenate(
        [col_shift[pl.ds(row_of(j, t), 1), :] for j in range(2) for t in range(4)], axis=1
    )
    row_tail[...] = in_parts(
        (jnp.sum(row_lse, keepdims=True) - 2.0 * picked) * LN2,
        (jnp.sum(row_mean, keepdims=True) - 2.0 * picked) * LN2,
    )
    col_tail[...] = in_parts(
        jnp.sum(col_lse, keepdims=True) * LN2, jnp.sum(col_mean, keepdims=True) * LN2
    )


def images_grad(scale_ref, col_tail, t0, t1, d_ref, g_ref):
    product = jnp.dot(d_ref[:, :QUAD], t0[...], preferred_element_type=F32)
    product += jnp.dot(d_ref[:, QUAD:], t1[...], preferred_element_type=F32)
    g_ref[0:QUAD, :] = (scale_ref[0] * product).astype(BF16)
    g_ref[QUAD : QUAD + EXTRA, :] = col_tail[...]


def dlogit_kernel(pieces, ids_ref, scale_ref, *refs):
    either_way(scale_ref, lambda bounded: dlogit_part(bounded, pieces, ids_ref, *refs))


def dlogit_part(bounded, places_of, ids_ref, pos_ref, row_shift, col_shift, *refs):
    count = len(places_of)
    col_of, row_of = places(ids_ref)
    columns = jnp.exp2(-col_shift[...]) if bounded else col_shift[...]
    lanes = lax.broadcasted_iota(jnp.int32, (1, 8 * ROWS), 1)
    for q, kept_ref, d_ref in zip(places_of, refs[:count], refs[count:]):
        for h in range(QUAD // CHUNK):
            kept = kept_ref[h * CHUNK : (h + 1) * CHUNK, :]
            pieces = []
            for b in range(CHUNK // ROWS):
                place = col_of(q, h * (CHUNK // ROWS) + b)
                shift = row_shift[pl.ds(place, 1), :]
                shift = jnp.exp2(-shift) if bounded else shift
                shift = jnp.transpose(jnp.broadcast_to(shift, (ROWS, ROWS)))
                pos = pos_ref[pl.ds(pl.multiple_of(place * ROWS, ROWS), ROWS), :]
                shift = jnp.concatenate([shift] * 8, axis=1)
                pos = jnp.concatenate([pos] * 8, axis=1)
                part = kept[b * ROWS : (b + 1) * ROWS]
                if bounded:
                    soft = part * (shift + columns)
                else:
                    soft = jnp.exp2(part - shift) + jnp.exp2(part - columns)
                pieces.append(jnp.where(pos == lanes, soft - 1.0, soft).astype(BF16))
            d_ref[h * CHUNK : (h + 1) * CHUNK, :] = jnp.concatenate(pieces, axis=0)


def texts_grad_kernel(scale_ref, row_tail, i0, i1, i2, i3, d0, d1, d2, d3, *refs, j):
    out = refs[-1]
    rows = jnp.concatenate([r[...] for r in (i0, i1, i2, i3)], axis=0)
    part = jnp.concatenate([d[:, j * QUAD : (j + 1) * QUAD] for d in (d0, d1, d2, d3)], axis=0)
    update = lax.dot_general(rows, part, (((0,), (0,)), ((), ())), preferred_element_type=F32)
    out[0:QUAD, :] = (scale_ref[0] * jnp.transpose(update)).astype(BF16)
    out[QUAD : QUAD + EXTRA, :] = row_tail[...]


def tail_sum(refs, first):
    total = sum(r[first : first + EXTRA, :].astype(F32) for r in refs)
    total = jnp.sum(total, axis=0, keepdims=True)
    return total[:, 0:1], total[:, 1:2]


def partial_kernel(*refs):
    sources, outs = refs[:-4], refs[-4:]
    tail = in_parts(*tail_sum(sources, QUAD))
    for t, out in enumerate(outs):
        rows = slice(t * ROWS, (t + 1) * ROWS)
        out[0:ROWS, :] = sum(r[rows, :].astype(F32) for r in sources).astype(BF16)
        out[ROWS : ROWS + EXTRA, :] = tail


def finish_kernel(batch, img_ref, txt_ref, a0, a1, a2, a3, b0, b1, b2, b3, img_out, txt_out, loss_out, temp_out):
    for raw, parts, out in ((img_ref, (a0, a1, a2, a3), img_out), (txt_ref, (b0, b1, b2, b3), txt_out)):
        unit, inverse = unit_rows(raw[...])
        grad = sum(p[0:ROWS, :].astype(F32) for p in parts)
        out[...] = inverse * (grad - unit * jnp.sum(unit * grad, axis=1, keepdims=True))
    cols = tail_sum((a0, a1, a2, a3), ROWS)
    rows = tail_sum((b0, b1, b2, b3), ROWS)
    loss_out[0] = jnp.sum(cols[0] + rows[0]) / (2 * batch)
    temp_out[0] = jnp.sum(cols[1] + rows[1]) / (2 * batch)


def gathered(value, moves):
    return [value] + [shifted(value, moves(by)) for by in OFFS[1:]]


def scattered(parts, moves):
    return [parts[0]] + [shifted(p, moves(-by)) for p, by in zip(parts[1:], OFFS[1:])]


def across(place, far):
    return 3 - place if far else place ^ 1


def pair_b(far):
    return lambda z, k, x, y: (z, k, across(x, far), y) if k else (z, k, x, across(y, far))


def pair_z(far):
    return lambda z, k, x, y: (across(z, far), k, x, y)


def on_device(images, texts, partner, log_scale):
    row, col = lax.axis_index("row"), lax.axis_index("col")
    ids = jnp.stack([row, col]).astype(jnp.int32)
    scale = jnp.exp(log_scale)
    unit = shape((ROWS, WIDTH), BF16)
    anywhere = pl.BlockSpec(memory_space=pl.ANY)
    anywhere = pl.BlockSpec(memory_space=pl.ANY)
    token = shape((8, ROWS), F32)
    unit_img = call(unit_kernel, unit, images)
    unit_txt = call(unit_kernel, unit, texts, unit_img, specs=[VMEM, anywhere])
    img_own = jnp.concatenate(gathered(unit_img, ring_a), axis=0)
    txt0 = jnp.concatenate(gathered(unit_txt, ring_z), axis=0)
    imgs = gathered(img_own, ring_b)
    txt1 = shifted(txt0, other_core)
    arrived = call(after_kernel, token, imgs[3])

    owner = partner // (16 * ROWS)
    steps = (row // 2 - owner // 2) % 4
    slot = steps ^ (steps // 2)
    core = jnp.where(owner % 2 == row % 2, 0, 1)
    pos = (core * 4 + slot) * ROWS + partner % ROWS
    pos = jnp.where(partner // ROWS % 16 == col, pos, -1)
    pos = jnp.broadcast_to(pos[:, None], (16 * ROWS, ROWS))

    row_shape = shape((40, ROWS), F32)
    common = (ids, scale, pos)
    kept = shape((QUAD, 8 * ROWS), F32)
    row_stat, state, *near_kept = call(
        functools.partial(forward_kernel, False, (0, 3)),
        [row_shape, shape((8, 8 * ROWS), F32), kept, kept],
        *common, imgs[0], imgs[3], txt0, txt1, arrived, specs=[SMEM, SMEM] + [VMEM] * 6,
    )
    row_stat, col_stat, *far_kept = call(
        functools.partial(forward_kernel, True, (2, 1)),
        [row_shape, shape((48, ROWS), F32), kept, kept],
        *common, imgs[2], imgs[1], txt0, txt1, row_stat, state, specs=[SMEM, SMEM] + [VMEM] * 7,
    )
    kept = (near_kept[0], far_kept[1], far_kept[0], near_kept[1])
    col_shape = shape((48, ROWS), F32)
    row_stat, col_stat = call(
        merge_kernel, [row_shape, col_shape],
        *gathered(row_stat, ring_a), col_stat, shifted(col_stat, other_core),
    )
    row_stat, col_stat = call(
        merge_kernel, [row_shape, col_shape],
        row_stat, shifted(row_stat, pair_b(False)), col_stat, shifted(col_stat, pair_z(False)),
    )
    tail = shape((EXTRA, WIDTH), BF16)
    row_shift, col_shift, row_tail, col_tail = call(
        shifts_kernel, [shape((16, ROWS), F32), shape((1, 8 * ROWS), F32), tail, tail],
        ids, row_stat, shifted(row_stat, pair_b(True)), col_stat, shifted(col_stat, pair_z(True)),
        specs=[SMEM] + [VMEM] * 4, scratch=[pltpu.VMEM((8, ROWS), F32)],
    )

    sent = shape((QUAD + EXTRA, WIDTH), BF16)
    small = [shape((ROWS + EXTRA, WIDTH), BF16)] * 4
    dlogits = {}
    for pieces in ((3,), (2, 1, 0)):
        made = call(
            functools.partial(dlogit_kernel, pieces), [shape((QUAD, 8 * ROWS), BF16)] * len(pieces),
            *common, row_shift, col_shift, *(kept[q] for q in pieces),
            cost=BUSY, specs=[SMEM, SMEM] + [VMEM] * (3 + len(pieces)),
        )
        dlogits.update(zip(pieces, made))
    dlogits = [dlogits[q] for q in range(4)]
    grads = [
        call(images_grad, sent, scale, col_tail, txt0, txt1, d, cost=BUSY, specs=[SMEM] + [VMEM] * 4)
        for d in dlogits
    ]
    texts_args = (scale, row_tail, *imgs, *dlogits)
    txt_other = call(
        functools.partial(texts_grad_kernel, j=1), sent, *texts_args, *grads[1:],
        cost=BUSY, specs=[SMEM] + [VMEM] * 12,
    )
    txt_own = call(
        functools.partial(texts_grad_kernel, j=0), sent, *texts_args, txt_other,
        cost=BUSY, specs=[SMEM] + [VMEM] * 10,
    )
    txt_parts = call(
        partial_kernel, small, txt_own, shifted(txt_other, other_core)
    )
    txt_parts = scattered(txt_parts, ring_z)
    img_parts = call(
        lambda _, *refs: partial_kernel(*refs), small, txt_parts[0], *scattered(grads, ring_b),
        specs=[anywhere] + [VMEM] * 4,
    )
    img_parts = scattered(img_parts, ring_a)
    whole = shape((ROWS, WIDTH), F32)
    one = shape((1,), F32)
    return pl.pallas_call(
        functools.partial(finish_kernel, 128 * ROWS),
        out_shape=(whole, whole, one, one),
        in_specs=[VMEM] * 10,
        out_specs=(VMEM, VMEM, SMEM, SMEM),
        compiler_params=PARAMS,
    )(images, texts, *img_parts, *txt_parts)


def solution(mesh):
    placed = (P(("row", "col"), None), P(("row", "col"), None), P("row"), P())
    return jax.shard_map(
        on_device,
        mesh=mesh,
        in_specs=placed,
        out_specs=(P(("row", "col"), None), P(("row", "col"), None), P(), P()),
        check_vma=False,
    )
```

```python
import functools

import jax
import jax.numpy as jnp
from jax import lax
from jax.experimental import pallas as pl
from jax.experimental.pallas import tpu as pltpu
from jax.sharding import PartitionSpec as P

ROWS = 128
WIDTH = 512
QUAD = 4 * ROWS
EXTRA = 16
OFFS = (0, 1, 3, 2)
LOG2E = 1.4426950408889634
LN2 = 0.6931471805599453
RC = ("row", "col")
F32 = jnp.float32
BF16 = jnp.bfloat16
VMEM = pl.BlockSpec(memory_space=pltpu.VMEM)
SMEM = pl.BlockSpec(memory_space=pltpu.SMEM)
BUSY = pl.CostEstimate(flops=10**10, bytes_accessed=10**6, transcendentals=0)
PARAMS = pltpu.CompilerParams(vmem_limit_bytes=12 * 1024 * 1024)


def device(z, k, x, y):
    return (z * 2 + k) * 16 + x * 4 + y


def shifted(value, move):
    pairs = []
    for z in range(4):
        for k in range(2):
            for x in range(4):
                for y in range(4):
                    pairs.append((device(z, k, x, y), device(*move(z, k, x, y))))
    return lax.ppermute(value, RC, pairs)


def ring_a(by):
    return lambda z, k, x, y: (z, k, x, (y + by) % 4) if k else (z, k, (x + by) % 4, y)


def ring_b(by):
    return lambda z, k, x, y: (z, k, (x + by) % 4, y) if k else (z, k, x, (y + by) % 4)


def ring_z(by):
    return lambda z, k, x, y: ((z + by) % 4, k, x, y)


def other_core(z, k, x, y):
    return (z, 1 - k, x, y)


def call(kernel, outs, *args, specs=None, cost=None, scratch=()):
    return pl.pallas_call(
        kernel,
        out_shape=outs,
        in_specs=specs or [VMEM] * len(args),
        out_specs=jax.tree.map(lambda o: VMEM, outs),
        scratch_shapes=scratch,
        compiler_params=PARAMS,
        cost_estimate=cost,
    )(*args)


def shape(dims, dtype):
    return jax.ShapeDtypeStruct(dims, dtype)


def unit_rows(values):
    widened = values.astype(F32)
    inverse = lax.rsqrt(jnp.sum(widened * widened, axis=1, keepdims=True) + 1e-06)
    return widened * inverse, inverse


def unit_kernel(raw_ref, *refs):
    refs[-1][...] = unit_rows(raw_ref[...])[0].astype(BF16)


def after_kernel(*refs):
    refs[-1][...] = jnp.zeros_like(refs[-1])


def places(ids_ref):
    row, col = ids_ref[0], ids_ref[1]
    z, k, x, y = row // 2, row % 2, col // 4, col % 4
    pos_a = jnp.where(k == 0, x, y)
    pos_b = jnp.where(k == 0, y, x)

    def col_of(q, a):
        in_b = (pos_b + 4 - OFFS[q]) % 4
        in_a = (pos_a + 4 - OFFS[a]) % 4
        return jnp.where(k == 0, in_a * 4 + in_b, in_b * 4 + in_a)

    def row_of(j, t):
        return (z + 4 - OFFS[t]) % 4 * 2 + (k if j == 0 else 1 - k)

    return col_of, row_of


def to_lanes(column):
    return jnp.transpose(jnp.broadcast_to(column, (ROWS, ROWS)))[0:1, :]


def logits2(rows, t0, t1, scale2):
    parts = [
        lax.dot_general(rows, t[...], (((1,), (1,)), ((), ())), preferred_element_type=F32)
        for t in (t0, t1)
    ]
    return jnp.concatenate(parts, axis=1) * scale2


CHUNK = 256


def either_way(scale_ref, part):
    bounded = scale_ref[0] * (LOG2E * 1.01) <= 100.0
    pl.when(bounded)(functools.partial(part, True))
    pl.when(jnp.logical_not(bounded))(functools.partial(part, False))


def forward_kernel(last, places_of, ids_ref, scale_ref, *refs):
    either_way(
        scale_ref, lambda bounded: forward_part(bounded, last, places_of, ids_ref, scale_ref, *refs)
    )


def lane_sums(values):
    part = sum(values[:, c * ROWS : (c + 1) * ROWS] for c in range(8))
    return jnp.sum(jnp.transpose(part), axis=0, keepdims=True)


def forward_part(bounded, last, places_of, ids_ref, scale_ref, pos_ref, i0, i1, t0, t1, *refs):
    scale2 = scale_ref[0] * LOG2E
    col_of, row_of = places(ids_ref)
    lanes = lax.broadcasted_iota(jnp.int32, (1, 8 * ROWS), 1)
    if last:
        row_in, state_in, row_out, col_out, *kept = refs
        row_out[...] = row_in[...]
        col_high, col_total, col_weighted, picked = (state_in[i : i + 1, :] for i in range(4))
    else:
        _, row_out, state_out, *kept = refs
        col_high = jnp.full((1, 8 * ROWS), 0.0 if bounded else -jnp.inf, F32)
        col_total = col_weighted = picked = jnp.zeros((1, 8 * ROWS), F32)
    for q, rows_ref, kept_ref in zip(places_of, (i0, i1), kept):
        for h in range(QUAD // CHUNK):
            logits = logits2(rows_ref[h * CHUNK : (h + 1) * CHUNK, :], t0, t1, scale2)
            if bounded:
                weights = jnp.exp2(logits)
                kept_ref[h * CHUNK : (h + 1) * CHUNK, :] = weights
                weighted = weights * logits
                col_total += jnp.sum(weights, axis=0, keepdims=True)
                col_weighted += jnp.sum(weighted, axis=0, keepdims=True)
            else:
                kept_ref[h * CHUNK : (h + 1) * CHUNK, :] = logits
                high = jnp.max(logits, axis=1, keepdims=True)
                weights = jnp.exp2(logits - high)
                total = jnp.sum(weights, axis=1, keepdims=True)
                mean = jnp.sum(weights * logits, axis=1, keepdims=True) / total
                lse = high + jnp.log2(total)
                old = col_high
                col_high = jnp.maximum(old, jnp.max(logits, axis=0, keepdims=True))
                rescale = jnp.exp2(old - col_high)
                weights = jnp.exp2(logits - col_high)
                col_total = col_total * rescale + jnp.sum(weights, axis=0, keepdims=True)
                col_weighted = col_weighted * rescale + jnp.sum(
                    weights * logits, axis=0, keepdims=True
                )
            pos = []
            for b in range(CHUNK // ROWS):
                place = col_of(q, h * (CHUNK // ROWS) + b)
                block = slice(b * ROWS, (b + 1) * ROWS)
                if bounded:
                    total = lane_sums(weights[block])
                    row_out[pl.ds(place, 1), :] = jnp.log2(total)
                    row_out[pl.ds(16 + place, 1), :] = lane_sums(weighted[block]) / total
                else:
                    row_out[pl.ds(place, 1), :] = to_lanes(lse[block])
                    row_out[pl.ds(16 + place, 1), :] = to_lanes(mean[block])
                pos.append(pos_ref[pl.ds(pl.multiple_of(place * ROWS, ROWS), ROWS), :])
            pos = jnp.concatenate(pos, axis=0)
            pos = jnp.concatenate([pos] * 8, axis=1)
            picked += jnp.sum(jnp.where(pos == lanes, logits, 0.0), axis=0, keepdims=True)
    if not last:
        for i, value in enumerate((col_high, col_total, col_weighted, picked)):
            state_out[i : i + 1, :] = value
        return
    row_out[32:40, :] = jnp.broadcast_to(jnp.sum(picked, axis=1, keepdims=True), (8, ROWS))
    col_out[16:, :] = jnp.zeros_like(col_out[16:, :])
    col_lse = col_high + jnp.log2(col_total)
    col_mean = col_weighted / col_total
    for j in range(2):
        for t in range(4):
            at = (j * 4 + t) * ROWS
            place = row_of(j, t)
            col_out[pl.ds(place, 1), :] = col_lse[:, at : at + ROWS]
            col_out[pl.ds(8 + place, 1), :] = col_mean[:, at : at + ROWS]


def merged(parts, count):
    lse = [p[0:count, :] for p in parts]
    high = functools.reduce(jnp.maximum, lse)
    weights = [jnp.exp2(p - high) for p in lse]
    total = sum(weights)
    mean = sum(w * p[count : 2 * count, :] for w, p in zip(weights, parts)) / total
    return high + jnp.log2(total), mean


def merge_kernel(*refs):
    *refs, c0, c1, row_out, col_out = refs
    row_out[0:16, :], row_out[16:32, :] = merged(refs, 16)
    row_out[32:40, :] = sum(r[32:40, :] for r in refs)
    col_out[0:8, :], col_out[8:16, :] = merged((c0, c1), 8)
    col_out[16:, :] = jnp.zeros_like(col_out[16:, :])


def in_parts(first, second):
    lane = lax.broadcasted_iota(jnp.int32, (EXTRA, WIDTH), 1)
    part = lax.broadcasted_iota(jnp.int32, (EXTRA, WIDTH), 0)
    value = jnp.where(lane == 0, first, jnp.where(lane == 1, second, 0.0))
    high = value.astype(BF16)
    rest = value - high.astype(F32)
    mid = rest.astype(BF16)
    low = (rest - mid.astype(F32)).astype(BF16)
    zero = jnp.zeros((EXTRA, WIDTH), F32)
    out = jnp.where(part == 0, high.astype(F32), zero)
    out = jnp.where(part == 1, mid.astype(F32), out)
    return jnp.where(part == 2, low.astype(F32), out).astype(BF16)


def shifts_kernel(ids_ref, r0, r1, c0, c1, row_shift, columns, row_tail, col_tail, col_shift):
    _, row_of = places(ids_ref)
    row_lse, row_mean = merged((r0, r1), 16)
    col_lse, col_mean = merged((c0, c1), 8)
    picked = r0[32:33, 0:1] + r1[32:33, 0:1]
    row_shift[...] = row_lse + 1.0
    col_shift[...] = col_lse + 1.0
    columns[...] = jnp.concatenate(
        [col_shift[pl.ds(row_of(j, t), 1), :] for j in range(2) for t in range(4)], axis=1
    )
    row_tail[...] = in_parts(
        (jnp.sum(row_lse, keepdims=True) - 2.0 * picked) * LN2,
        (jnp.sum(row_mean, keepdims=True) - 2.0 * picked) * LN2,
    )
    col_tail[...] = in_parts(
        jnp.sum(col_lse, keepdims=True) * LN2, jnp.sum(col_mean, keepdims=True) * LN2
    )


def images_grad(scale_ref, col_tail, t0, t1, d_ref, g_ref):
    product = jnp.dot(d_ref[:, :QUAD], t0[...], preferred_element_type=F32)
    product += jnp.dot(d_ref[:, QUAD:], t1[...], preferred_element_type=F32)
    g_ref[0:QUAD, :] = (scale_ref[0] * product).astype(BF16)
    g_ref[QUAD : QUAD + EXTRA, :] = col_tail[...]


def dlogit_kernel(pieces, ids_ref, scale_ref, *refs):
    either_way(scale_ref, lambda bounded: dlogit_part(bounded, pieces, ids_ref, *refs))


def dlogit_part(bounded, places_of, ids_ref, pos_ref, row_shift, col_shift, *refs):
    count = len(places_of)
    col_of, row_of = places(ids_ref)
    columns = jnp.exp2(-col_shift[...]) if bounded else col_shift[...]
    lanes = lax.broadcasted_iota(jnp.int32, (1, 8 * ROWS), 1)
    for q, kept_ref, d_ref in zip(places_of, refs[:count], refs[count:]):
        for h in range(QUAD // CHUNK):
            kept = kept_ref[h * CHUNK : (h + 1) * CHUNK, :]
            pieces = []
            for b in range(CHUNK // ROWS):
                place = col_of(q, h * (CHUNK // ROWS) + b)
                shift = row_shift[pl.ds(place, 1), :]
                shift = jnp.exp2(-shift) if bounded else shift
                shift = jnp.transpose(jnp.broadcast_to(shift, (ROWS, ROWS)))
                pos = pos_ref[pl.ds(pl.multiple_of(place * ROWS, ROWS), ROWS), :]
                shift = jnp.concatenate([shift] * 8, axis=1)
                pos = jnp.concatenate([pos] * 8, axis=1)
                part = kept[b * ROWS : (b + 1) * ROWS]
                if bounded:
                    soft = part * (shift + columns)
                else:
                    soft = jnp.exp2(part - shift) + jnp.exp2(part - columns)
                pieces.append(jnp.where(pos == lanes, soft - 1.0, soft).astype(BF16))
            d_ref[h * CHUNK : (h + 1) * CHUNK, :] = jnp.concatenate(pieces, axis=0)


def texts_grad_kernel(scale_ref, row_tail, i0, i1, i2, i3, d0, d1, d2, d3, *refs, j):
    out = refs[-1]
    rows = jnp.concatenate([r[...] for r in (i0, i1, i2, i3)], axis=0)
    part = jnp.concatenate([d[:, j * QUAD : (j + 1) * QUAD] for d in (d0, d1, d2, d3)], axis=0)
    update = lax.dot_general(rows, part, (((0,), (0,)), ((), ())), preferred_element_type=F32)
    out[0:QUAD, :] = (scale_ref[0] * jnp.transpose(update)).astype(BF16)
    out[QUAD : QUAD + EXTRA, :] = row_tail[...]


def tail_sum(refs, first):
    total = sum(r[first : first + EXTRA, :].astype(F32) for r in refs)
    total = jnp.sum(total, axis=0, keepdims=True)
    return total[:, 0:1], total[:, 1:2]


def partial_kernel(*refs):
    sources, outs = refs[:-4], refs[-4:]
    tail = in_parts(*tail_sum(sources, QUAD))
    for t, out in enumerate(outs):
        rows = slice(t * ROWS, (t + 1) * ROWS)
        out[0:ROWS, :] = sum(r[rows, :].astype(F32) for r in sources).astype(BF16)
        out[ROWS : ROWS + EXTRA, :] = tail


def finish_kernel(batch, img_ref, txt_ref, a0, a1, a2, a3, b0, b1, b2, b3, img_out, txt_out, loss_out, temp_out):
    for raw, parts, out in ((img_ref, (a0, a1, a2, a3), img_out), (txt_ref, (b0, b1, b2, b3), txt_out)):
        unit, inverse = unit_rows(raw[...])
        grad = sum(p[0:ROWS, :].astype(F32) for p in parts)
        out[...] = inverse * (grad - unit * jnp.sum(unit * grad, axis=1, keepdims=True))
    cols = tail_sum((a0, a1, a2, a3), ROWS)
    rows = tail_sum((b0, b1, b2, b3), ROWS)
    loss_out[0] = jnp.sum(cols[0] + rows[0]) / (2 * batch)
    temp_out[0] = jnp.sum(cols[1] + rows[1]) / (2 * batch)


def gathered(value, moves):
    return [value] + [shifted(value, moves(by)) for by in OFFS[1:]]


def scattered(parts, moves):
    return [parts[0]] + [shifted(p, moves(-by)) for p, by in zip(parts[1:], OFFS[1:])]


def across(place, far):
    return 3 - place if far else place ^ 1


def pair_b(far):
    return lambda z, k, x, y: (z, k, across(x, far), y) if k else (z, k, x, across(y, far))


def pair_z(far):
    return lambda z, k, x, y: (across(z, far), k, x, y)


def on_device(images, texts, partner, log_scale):
    row, col = lax.axis_index("row"), lax.axis_index("col")
    ids = jnp.stack([row, col]).astype(jnp.int32)
    scale = jnp.exp(log_scale)
    unit = shape((ROWS, WIDTH), BF16)
    anywhere = pl.BlockSpec(memory_space=pl.ANY)
    anywhere = pl.BlockSpec(memory_space=pl.ANY)
    token = shape((8, ROWS), F32)
    unit_img = call(unit_kernel, unit, images)
    unit_txt = call(unit_kernel, unit, texts)
    img_own = jnp.concatenate(gathered(unit_img, ring_a), axis=0)
    txt0 = jnp.concatenate(gathered(unit_txt, ring_z), axis=0)
    imgs = gathered(img_own, ring_b)
    txt1 = shifted(txt0, other_core)
    arrived = call(after_kernel, token, imgs[3])

    owner = partner // (16 * ROWS)
    steps = (row // 2 - owner // 2) % 4
    slot = steps ^ (steps // 2)
    core = jnp.where(owner % 2 == row % 2, 0, 1)
    pos = (core * 4 + slot) * ROWS + partner % ROWS
    pos = jnp.where(partner // ROWS % 16 == col, pos, -1)
    pos = jnp.broadcast_to(pos[:, None], (16 * ROWS, ROWS))

    row_shape = shape((40, ROWS), F32)
    common = (ids, scale, pos)
    kept = shape((QUAD, 8 * ROWS), F32)
    row_stat, state, *near_kept = call(
        functools.partial(forward_kernel, False, (0, 3)),
        [row_shape, shape((8, 8 * ROWS), F32), kept, kept],
        *common, imgs[0], imgs[3], txt0, txt1, arrived, specs=[SMEM, SMEM] + [VMEM] * 6,
    )
    row_stat, col_stat, *far_kept = call(
        functools.partial(forward_kernel, True, (2, 1)),
        [row_shape, shape((48, ROWS), F32), kept, kept],
        *common, imgs[2], imgs[1], txt0, txt1, row_stat, state, specs=[SMEM, SMEM] + [VMEM] * 7,
    )
    kept = (near_kept[0], far_kept[1], far_kept[0], near_kept[1])
    col_shape = shape((48, ROWS), F32)
    row_stat, col_stat = call(
        merge_kernel, [row_shape, col_shape],
        *gathered(row_stat, ring_a), col_stat, shifted(col_stat, other_core),
    )
    row_stat, col_stat = call(
        merge_kernel, [row_shape, col_shape],
        row_stat, shifted(row_stat, pair_b(False)), col_stat, shifted(col_stat, pair_z(False)),
    )
    tail = shape((EXTRA, WIDTH), BF16)
    row_shift, col_shift, row_tail, col_tail = call(
        shifts_kernel, [shape((16, ROWS), F32), shape((1, 8 * ROWS), F32), tail, tail],
        ids, row_stat, shifted(row_stat, pair_b(True)), col_stat, shifted(col_stat, pair_z(True)),
        specs=[SMEM] + [VMEM] * 4, scratch=[pltpu.VMEM((8, ROWS), F32)],
    )

    sent = shape((QUAD + EXTRA, WIDTH), BF16)
    small = [shape((ROWS + EXTRA, WIDTH), BF16)] * 4
    dlogits = {}
    for pieces in ((3,), (2, 1, 0)):
        made = call(
            functools.partial(dlogit_kernel, pieces), [shape((QUAD, 8 * ROWS), BF16)] * len(pieces),
            *common, row_shift, col_shift, *(kept[q] for q in pieces),
            cost=BUSY, specs=[SMEM, SMEM] + [VMEM] * (3 + len(pieces)),
        )
        dlogits.update(zip(pieces, made))
    dlogits = [dlogits[q] for q in range(4)]
    grads = [
        call(images_grad, sent, scale, col_tail, txt0, txt1, d, cost=BUSY, specs=[SMEM] + [VMEM] * 4)
        for d in dlogits
    ]
    texts_args = (scale, row_tail, *imgs, *dlogits)
    txt_other = call(
        functools.partial(texts_grad_kernel, j=1), sent, *texts_args, *grads[1:],
        cost=BUSY, specs=[SMEM] + [VMEM] * 12,
    )
    txt_own = call(
        functools.partial(texts_grad_kernel, j=0), sent, *texts_args, txt_other,
        cost=BUSY, specs=[SMEM] + [VMEM] * 10,
    )
    txt_parts = call(
        partial_kernel, small, txt_own, shifted(txt_other, other_core)
    )
    txt_parts = scattered(txt_parts, ring_z)
    img_parts = call(
        lambda _, *refs: partial_kernel(*refs), small, txt_parts[0], *scattered(grads, ring_b),
        specs=[anywhere] + [VMEM] * 4,
    )
    img_parts = scattered(img_parts, ring_a)
    whole = shape((ROWS, WIDTH), F32)
    one = shape((1,), F32)
    return pl.pallas_call(
        functools.partial(finish_kernel, 128 * ROWS),
        out_shape=(whole, whole, one, one),
        in_specs=[VMEM] * 10,
        out_specs=(VMEM, VMEM, SMEM, SMEM),
        compiler_params=PARAMS,
    )(images, texts, *img_parts, *txt_parts)


def solution(mesh):
    placed = (P(("row", "col"), None), P(("row", "col"), None), P("row"), P())
    return jax.shard_map(
        on_device,
        mesh=mesh,
        in_specs=placed,
        out_specs=(P(("row", "col"), None), P(("row", "col"), None), P(), P()),
        check_vma=False,
    )
```
